32 devices in a mesh: mesh: 8 (over z, y), comp: 4 (over x, core).
Axes of the slice: x: 2, y: 2, z: 4, core: 2. Of those that a mesh axis runs over, the one named last changes fastest.
Arguments:
- a_blocks: bfloat16 [1536, 64, 448], P(('mesh', 'comp')), may hold values from -0.25 to 0.25
- a_columns: int32 [1536, 7], P(('mesh', 'comp')), may hold values from 0 to 71, as said below
- p_blocks: bfloat16 [1536, 64, 192], P(('mesh', 'comp')), may hold values from -0.75 to 0.75
- p_columns: int32 [1536, 3], P(('mesh', 'comp')), may hold values from 0 to 3, all different within a row
- r_blocks: bfloat16 [1536, 64, 192], P(('mesh', 'comp')), may hold values from -0.75 to 0.75
- r_columns: int32 [1536, 3], P(('mesh', 'comp')), may hold values from 0 to 11, as said below
- sent_up: int32 [384], P(('mesh', 'comp')), may hold values from 0 to 47, as said below
- sent_down: int32 [384], P(('mesh', 'comp')), may hold values from 0 to 47, as said below
- vectors: bfloat16 [1536, 128], P(('mesh', 'comp')), may hold values from -2 to 2
- coarse_dest: int32 [128, 1], P(('mesh', 'comp')), may hold values from 0 to 3; in each aligned block of 4 rows (0 to 3, 4 to 7, ...) at most 2 rows name the same one
Outputs:
- coarse_matrix: bfloat16 [256, 64, 1280], P(('mesh', 'comp'))
- coarse_vectors: bfloat16 [256, 128], P(('mesh', 'comp'))
The draws below stay inside these ranges and needn't reach their ends.
Inputs may be any that keep to these rules, and one draw needn't show every extreme that they name: `a_columns`: each fine row's first column is the row itself (its own local number). A column 48 + i exists only on devices with a device below along mesh, 60 + i only on devices with one above; every listed ghost of an existing neighbour is named by some row. `r_columns`: h is never toward a device missing along mesh. Local row numbers; the 12 entries of one device in sent_up and in sent_down are distinct, and no row is in both lists. `sent_down`: see sent_up. `coarse_dest`: at most 2 of the 4 coarse rows of one home go to one owner comp, and that many do in some home. `p_columns`: the 3 entries of a row are distinct.
All inputs are finite; a program needn't handle non-finite values.
Results may differ from the reference program's by a relative error of at most 0.0049.
Values may be sent and summed in bfloat16 or wider, within the bound.
A program may use at most 128 MiB of HBM per device.

```python
import math
import jax
import jax.numpy as jnp
import numpy as np
from jax import lax

B = 64
KA = 7
KP = 3
KR = 3
NB = 48
NCL = 4
GH = 12
CAP = 2
W = 20
NF = 1536
NC = 128
OWN_SLOTS = 256
N_MESH = 8
N_COMP = 4
DEVICES = 32


def ghost_orders(key):
    keys = jax.random.split(key, DEVICES)
    return jax.vmap(lambda single: jax.random.permutation(single, NB))(keys).astype(jnp.int32)


def draw_sent_up(key, part):
    orders = ghost_orders(key)
    return orders[:, :GH].reshape(DEVICES * GH)


def draw_sent_down(key, part):
    orders = ghost_orders(key)
    return orders[:, GH:2 * GH].reshape(DEVICES * GH)


def draw_a_columns(key, part):
    key = jax.random.fold_in(key, 11)
    first_key, second_key, third_key, fourth_key = jax.random.split(key, 4)
    local = jax.random.randint(first_key, (DEVICES, NB, KA), 0, NB).astype(jnp.int32)
    local = local.at[:, :, 0].set(jnp.arange(NB, dtype=jnp.int32)[None, :])
    orders = jax.vmap(lambda single: jax.random.permutation(single, NB))(jax.random.split(second_key, DEVICES)).astype(jnp.int32)
    mesh_pos = jnp.arange(DEVICES, dtype=jnp.int32) // N_COMP
    choose_ghost = jax.random.randint(third_key, (DEVICES, NB, KA), 0, 6)
    ghost_pick = jax.random.randint(fourth_key, (DEVICES, NB, KA), 0, 2 * GH)
    allowed = jnp.where(ghost_pick < GH, mesh_pos[:, None, None] > 0, mesh_pos[:, None, None] < N_MESH - 1)
    later = jnp.arange(KA, dtype=jnp.int32)[None, None, :] >= 3
    local = jnp.where((choose_ghost == 0) & later & allowed, NB + ghost_pick, local).astype(jnp.int32)
    ghost_index = jnp.arange(GH, dtype=jnp.int32)

    def one_device(rows, order, position):
        low_rows = order[:GH]
        high_rows = order[GH:2 * GH]
        low_values = jnp.where(position > 0, NB + ghost_index, rows[low_rows, 1])
        high_values = jnp.where(position < N_MESH - 1, NB + GH + ghost_index, rows[high_rows, 2])
        rows = rows.at[low_rows, 1].set(low_values)
        return rows.at[high_rows, 2].set(high_values)
    return jax.vmap(one_device)(local, orders, mesh_pos).reshape(NF, KA).astype(jnp.int32)


def draw_r_columns(key, part):
    key = jax.random.fold_in(key, 31)
    first_key, second_key = jax.random.split(key)
    side = jax.random.randint(first_key, (DEVICES, NB, KR), 0, 3).astype(jnp.int32)
    mesh_pos = (jnp.arange(DEVICES, dtype=jnp.int32) // N_COMP)[:, None, None]
    side = jnp.where((mesh_pos == 0) & (side == 0), 1, side)
    side = jnp.where((mesh_pos == N_MESH - 1) & (side == 2), 1, side)
    within = jax.random.randint(second_key, (DEVICES, NB, KR), 0, NCL).astype(jnp.int32)
    return (side * NCL + within).reshape(NF, KR).astype(jnp.int32)


def steps_of(rng, dims, cuts, smallest, top_value):
    factor_of = 1.0
    for axis_at, parts in cuts:
        steps = jax.random.uniform(jax.random.fold_in(jax.random.fold_in(rng, 6), axis_at), (parts,), jnp.float32, smallest / len(cuts), top_value / len(cuts))
        factor_of = factor_of * jnp.repeat(jnp.exp(steps), dims[axis_at] // parts).reshape((-1,) + (1,) * (len(dims) - 1 - axis_at))
    return factor_of


def different_ones(stream_key, rows, amount, top, lift):
    order = jax.random.permutation(jax.random.fold_in(stream_key, 1), amount)
    boost = order
    for power in range(3):
        boost = boost * boost // amount
    boost = boost * lift // amount
    chance = jax.random.randint(jax.random.fold_in(stream_key, 2), (rows, amount), 0, 4096) + boost
    fixed_rows = jax.random.permutation(jax.random.fold_in(stream_key, 3), rows)[jnp.arange(amount) % rows]
    chance = jnp.where(jnp.arange(rows)[:, None] == fixed_rows[None, :], 1 << 14, chance)
    merit = chance * amount + jnp.arange(amount)
    return lax.top_k(merit.astype(jnp.int32), top)[1].astype(jnp.int32)


def shared_out(key, own, number, rows, number_of, top, reach, slope):
    order = jax.random.permutation(key, number_of)
    heavy_load, ordinary = load_shares(number_of, rows * top, reach, slope, True), load_shares(number_of, rows * top, reach, slope, False)
    places = jnp.arange(number_of)

    def named(lengths, offset_by):
        used = int((lengths > 0).sum())
        fixed = max(1, used // 4)
        shifted = fixed + (places - fixed + offset_by * (used - fixed)) % max(1, number_of - fixed)
        return jnp.zeros((number_of,), jnp.int32).at[order[jnp.where(places < fixed, places, shifted)]].set(jnp.asarray(lengths, jnp.int32))

    lengths = jnp.where(number % 4 == 0, named(heavy_load, number // 4), named(ordinary, number - number // 4 - 1))
    mixed = jax.random.permutation(jax.random.fold_in(own, 3), number_of)
    source_of, receiver = mixed[0:number_of // 2 * 2:2], mixed[1:number_of // 2 * 2:2]
    slack = jnp.minimum(lengths[source_of] - 1, reach - lengths[receiver]) // 2
    slack = jnp.where((source_of == order[0]) | (receiver == order[0]) | (lengths[receiver] == 0), 0, jnp.maximum(slack, 0))
    shifted = jax.random.randint(jax.random.fold_in(own, 4), (number_of // 2,), 0, 1 << 20) % (slack + 1)
    lengths = lengths.at[source_of].add(-shifted).at[receiver].add(shifted)
    labels = jnp.searchsorted(jnp.cumsum(lengths), jnp.arange(rows * top), side="right").astype(jnp.int32)
    table = labels.reshape(top, rows).T
    table = table[jax.random.permutation(jax.random.fold_in(own, 1), rows)]
    offset_by = jax.random.randint(jax.random.fold_in(own, 2), (rows, 1), 0, top)
    return jnp.take_along_axis(table, (jnp.arange(top)[None, :] + offset_by) % top, axis=1)


def load_shares(number_of, total, bound, slope, full):
    portions = [(1 << 20) // math.isqrt(rank ** slope) + 1 for rank in range(1, number_of + 1)]
    largest = bound if full else min(bound, max(-(-total // number_of), total * portions[0] // sum(portions)))
    least = 1 if total - largest >= number_of - 1 else 0
    given, rest = [largest] + [least] * (number_of - 1), total - largest - least * (number_of - 1)
    while rest > 0:
        free = [i for i in range(1, number_of) if given[i] < largest] or [i for i in range(1, number_of) if given[i] < bound]
        pool, remaining = sum([portions[i] for i in free]), rest
        for i in free:
            extra = min(bound - given[i], max(1, remaining * portions[i] // pool), rest)
            given[i] = given[i] + extra
            rest = rest - extra
    return np.array(given)


def noise(key, shape, width, bound, cuts=(), kind=jnp.bfloat16):
    level = steps_of(key, shape, cuts, -0.22, 0.18) if cuts else 1.0
    array = jax.random.normal(key, shape, jnp.float32) * width * level
    return jnp.minimum(jnp.maximum(array, -bound), bound).astype(kind)


def setup_inputs(seed: int = 0) -> dict:
    splits = jax.random.split(jax.random.key(seed), 11)
    a_blocks = noise(splits[0], (NF, B, KA * B), (KA * B) ** -0.5, 0.25, ((0, 32),))
    a_columns = draw_a_columns(jax.random.fold_in(splits[10], 71), 0)
    p_blocks = noise(splits[2], (NF, B, KP * B), B ** -0.5, 0.75, ((0, 32),))
    p_columns = different_ones(splits[3], NF, NCL, KP, 0)
    r_blocks = noise(splits[4], (NF, B, KR * B), B ** -0.5, 0.75, ((0, 32),))
    r_columns = draw_r_columns(jax.random.fold_in(splits[10], 71), 0)
    sent_up = draw_sent_up(jax.random.fold_in(splits[10], 71), 0)
    sent_down = draw_sent_down(jax.random.fold_in(splits[10], 71), 0)
    vectors = noise(splits[8], (NF, 2 * B), 0.25, 2.0, ((0, 32),))
    coarse_dest_keys = jax.random.split(jax.random.fold_in(splits[9], 1), NC // NCL)
    coarse_dest_turns = jax.random.permutation(jax.random.fold_in(splits[9], 3), NC // NCL)
    coarse_dest = jax.vmap(lambda own, number: shared_out(jax.random.fold_in(splits[9], 2), own, number, NCL, N_COMP, 1, CAP, 1))(coarse_dest_keys, coarse_dest_turns).reshape((NC, 1))
    return dict(a_blocks=a_blocks, a_columns=a_columns, p_blocks=p_blocks, p_columns=p_columns, r_blocks=r_blocks, r_columns=r_columns, sent_up=sent_up, sent_down=sent_down, vectors=vectors, coarse_dest=coarse_dest)


def densify(values, columns):
    count = values.shape[0]
    blocks = values.astype(jnp.float32).reshape(count, B, KP, B)
    onehot = (columns[:, :, None] == jnp.arange(NCL, dtype=jnp.int32)[None, None, :]).astype(jnp.float32)
    return jnp.einsum('rqs,rbqc->rbsc', onehot, blocks).reshape(count, B, NCL * B)


def widen(strip, offset):
    seg_width = NCL * B
    return jnp.pad(strip, ((0, 0), (0, 0), ((1 - offset) * seg_width, (1 + offset) * seg_width)))


def reference(a_blocks, a_columns, p_blocks, p_columns, r_blocks, r_columns, sent_up, sent_down, vectors, coarse_dest):
    def device_terms(device):
        mesh_pos = device // N_COMP
        lower = jnp.maximum(device - N_COMP, 0).astype(jnp.int32)
        upper = jnp.minimum(device + N_COMP, DEVICES - 1).astype(jnp.int32)
        first = (device * NB).astype(jnp.int32)
        a_rows = lax.dynamic_slice_in_dim(a_blocks, first, NB, 0).astype(jnp.float32)
        columns = lax.dynamic_slice_in_dim(a_columns, first, NB, 0)
        own_rows = densify(lax.dynamic_slice_in_dim(p_blocks, first, NB, 0), lax.dynamic_slice_in_dim(p_columns, first, NB, 0))
        low_ids = (lower * NB + lax.dynamic_slice_in_dim(sent_up, (lower * GH).astype(jnp.int32), GH, 0)).astype(jnp.int32)
        high_ids = (upper * NB + lax.dynamic_slice_in_dim(sent_down, (upper * GH).astype(jnp.int32), GH, 0)).astype(jnp.int32)
        low_rows = densify(p_blocks[low_ids], p_columns[low_ids]) * (mesh_pos > 0).astype(jnp.float32)
        high_rows = densify(p_blocks[high_ids], p_columns[high_ids]) * (mesh_pos < N_MESH - 1).astype(jnp.float32)
        p_table = jnp.concatenate([own_rows, low_rows, high_rows], 0)
        segment = jnp.where(columns < NB, 1, jnp.where(columns < NB + GH, 0, 2)).astype(jnp.int32)
        applied = jnp.zeros((NB, B, 3, NCL * B), jnp.float32)
        for k in range(KA):
            product = jnp.einsum('fab,fbc->fac', a_rows[:, :, k * B:(k + 1) * B], p_table[columns[:, k]])
            chooser = (segment[:, k][:, None] == jnp.arange(3, dtype=jnp.int32)[None, :]).astype(jnp.float32)
            applied = applied + product[:, :, None, :] * chooser[:, None, :, None]
        applied = applied.reshape(NB, B, 3 * NCL * B).astype(jnp.bfloat16)
        applied = lax.optimization_barrier(applied).astype(jnp.float32)
        r_rows = lax.dynamic_slice_in_dim(r_blocks, first, NB, 0).astype(jnp.float32)
        targets = lax.dynamic_slice_in_dim(r_columns, first, NB, 0)
        vec_rows = lax.dynamic_slice_in_dim(vectors, first, NB, 0).astype(jnp.float32).reshape(NB, 2, B)
        terms = jnp.zeros((3 * NCL, B, 3 * NCL * B), jnp.float32)
        vec_terms = jnp.zeros((3 * NCL, 2, B), jnp.float32)
        for j in range(KR):
            r_block = r_rows[:, :, j * B:(j + 1) * B]
            terms = terms.at[targets[:, j]].add(jnp.einsum('fab,fbx->fax', r_block, applied))
            vec_terms = vec_terms.at[targets[:, j]].add(jnp.einsum('fab,ftb->fta', r_block, vec_rows))
        return terms, vec_terms

    def accumulate(device, carry):
        coarse_sum, vec_sum = carry
        terms, vec_terms = device_terms(device)
        for offset in (-1, 0, 1):
            home = device + offset * N_COMP
            valid = ((home >= 0) & (home < DEVICES)).astype(jnp.float32)
            start = (jnp.clip(home, 0, DEVICES - 1) * NCL).astype(jnp.int32)
            piece = widen(terms[(offset + 1) * NCL:(offset + 2) * NCL], offset) * valid
            vec_piece = vec_terms[(offset + 1) * NCL:(offset + 2) * NCL] * valid
            current = lax.dynamic_slice_in_dim(coarse_sum, start, NCL, 0)
            coarse_sum = lax.dynamic_update_slice_in_dim(coarse_sum, current + piece, start, 0)
            vec_now = lax.dynamic_slice_in_dim(vec_sum, start, NCL, 0)
            vec_sum = lax.dynamic_update_slice_in_dim(vec_sum, vec_now + vec_piece, start, 0)
        return coarse_sum, vec_sum

    initial = (jnp.zeros((NC, B, W * B), jnp.float32), jnp.zeros((NC, 2, B), jnp.float32))
    coarse_sum, vec_sum = lax.fori_loop(jnp.int32(0), jnp.int32(DEVICES), accumulate, initial)
    home_of = jnp.arange(NC, dtype=jnp.int32) // NCL
    owner = coarse_dest[:, 0]
    onehot = (owner.reshape(DEVICES, NCL)[:, :, None] == jnp.arange(N_COMP, dtype=jnp.int32)[None, None, :]).astype(jnp.int32)
    ranking = jnp.sum((jnp.cumsum(onehot, 1).astype(jnp.int32) - onehot) * onehot, 2).astype(jnp.int32).reshape(NC)
    slots = ((((home_of // N_COMP) * N_COMP + owner) * N_COMP + home_of % N_COMP) * CAP + ranking).astype(jnp.int32)
    coarse_matrix = jnp.zeros((OWN_SLOTS, B, W * B), jnp.bfloat16).at[slots].set(coarse_sum.astype(jnp.bfloat16))
    coarse_vectors = jnp.zeros((OWN_SLOTS, 2 * B), jnp.bfloat16).at[slots].set(vec_sum.reshape(NC, 2 * B).astype(jnp.bfloat16))
    return coarse_matrix, coarse_vectors
```

```python
import functools

import jax
import jax.numpy as jnp
from jax import lax
from jax.experimental import pallas as pl
from jax.experimental.pallas import tpu as pltpu
from jax.sharding import PartitionSpec as P

MESH = pl.DeviceIdType.MESH
F32 = jnp.float32
BF16 = jnp.bfloat16
UNROLL = 4


def kernel(
    sizes,
    a_cols,
    p_cols,
    r_cols,
    up_rows,
    down_rows,
    dest,
    a_ref,
    p_ref,
    r_ref,
    vec_ref,
    out_ref,
    out_vec,
    eye,
    own,
    ghost,
    ghost_send,
    rd,
    appl,
    part_send,
    part_recv,
    own_part,
    rows,
    slots,
    vec_f32,
    vec_t,
    vpart_send,
    vpart_recv,
    vrows,
    vslots,
    vslots_recv,
    ghost_sems,
    part_sems,
    vpart_sems,
    slot_sems,
    local_sems,
    vslot_sems,
):
    mesh_count, comp_count, nf, width, ka, kp, kr, gh, nc, cap = sizes
    seg = nc * width
    m = lax.axis_index("mesh")
    c = lax.axis_index("comp")
    has_below = m > 0
    has_above = m < mesh_count - 1

    def along(step):
        return (m + step, c)

    def peer(r):
        return (m, lax.rem(c + r, comp_count))

    ghost[...] = jnp.zeros_like(ghost)
    part_recv[...] = jnp.zeros_like(part_recv)
    vpart_recv[...] = jnp.zeros_like(vpart_recv)

    barrier = pltpu.get_barrier_semaphore()
    for r in range(1, comp_count):
        pl.semaphore_signal(barrier, inc=1, device_id=peer(r), device_id_type=MESH)

    @pl.when(has_above)
    def _():
        pl.semaphore_signal(barrier, inc=1, device_id=along(1), device_id_type=MESH)

    @pl.when(has_below)
    def _():
        pl.semaphore_signal(barrier, inc=1, device_id=along(-1), device_id_type=MESH)

    lane = lax.broadcasted_iota(jnp.int32, (width, seg), 1)
    sub = lax.broadcasted_iota(jnp.int32, (width, seg), 0)
    eye[...] = jnp.where((lane & (width - 1)) == sub, 1.0, 0.0).astype(BF16)
    seg_lane = lax.broadcasted_iota(jnp.int32, (1, seg), 1)

    def dense_row(f):
        parts = []
        for q in range(kp):
            start = p_cols[f, q] * width
            hit = (seg_lane >= start) & (seg_lane < start + width)
            parts.append(eye[...] * jnp.where(hit, 1.0, 0.0).astype(BF16))
        spread = jnp.concatenate(parts, axis=0)
        return jnp.dot(p_ref[f], spread, preferred_element_type=F32).astype(BF16)

    def fill_ghosts(listed, at):
        def body(i, carry):
            for t in range(UNROLL):
                g = i * UNROLL + t
                ghost_send[at + g] = dense_row(listed[g])
            return carry

        lax.fori_loop(0, gh // UNROLL, body, 0)

    ghost_up = pltpu.make_async_remote_copy(
        src_ref=ghost_send.at[pl.ds(0, gh)],
        dst_ref=ghost.at[pl.ds(0, gh)],
        send_sem=ghost_sems.at[0],
        recv_sem=ghost_sems.at[1],
        device_id=along(1),
        device_id_type=MESH,
    )
    ghost_down = pltpu.make_async_remote_copy(
        src_ref=ghost_send.at[pl.ds(gh, gh)],
        dst_ref=ghost.at[pl.ds(gh, gh)],
        send_sem=ghost_sems.at[2],
        recv_sem=ghost_sems.at[3],
        device_id=along(-1),
        device_id_type=MESH,
    )
    fill_ghosts(up_rows, 0)
    pl.semaphore_wait(
        barrier,
        comp_count - 1 + jnp.where(has_below, 1, 0) + jnp.where(has_above, 1, 0),
    )

    @pl.when(has_above)
    def _():
        ghost_up.start()

    fill_ghosts(down_rows, gh)

    @pl.when(has_below)
    def _():
        ghost_down.start()

    def own_body(i, carry):
        for t in range(UNROLL):
            f = i * UNROLL + t
            own[f] = dense_row(f)
        return carry

    lax.fori_loop(0, nf // UNROLL, own_body, 0)

    vec_f32[...] = vec_ref[...].astype(F32)
    vec_t[...] = jnp.zeros_like(vec_t)
    pair_lane = lax.broadcasted_iota(jnp.int32, (1, 2 * width), 1)
    first_half = pair_lane < width

    def rd_body(i, carry):
        f = i * 2
        at = pl.ds(pl.multiple_of(i * 2 * width, 2 * width), 2 * width)
        even = r_ref[f]
        odd = r_ref[f + 1]
        blocks = []
        named = []
        for j in range(kr):
            cut = slice(j * width, (j + 1) * width)
            blocks.append(jnp.concatenate([even[:, cut], odd[:, cut]], axis=1))
            named.append(jnp.where(first_half, r_cols[f, j], r_cols[f + 1, j]))
        for target in range(3 * nc):
            total = None
            for j in range(kr):
                hit = jnp.where(named[j] == target, 1.0, 0.0).astype(BF16)
                term = blocks[j] * hit
                total = term if total is None else total + term
            rd[target * width : (target + 1) * width, at] = total
        v0 = vec_f32[pl.ds(f, 1), :]
        v1 = vec_f32[pl.ds(f + 1, 1), :]
        vec_t[0:1, at] = jnp.where(first_half, v0, pltpu.roll(v1, width, 1))
        vec_t[1:2, at] = jnp.where(first_half, pltpu.roll(v0, width, 1), v1)
        return carry

    lax.fori_loop(0, nf // 2, rd_body, 0)

    vec_part = lax.dot_general(
        vec_t[...].astype(BF16),
        rd[...],
        (((1,), (1,)), ((), ())),
        preferred_element_type=F32,
    )
    vpart_send[0] = vec_part[:, 0:seg]
    vpart_send[1] = vec_part[:, 2 * seg : 3 * seg]
    vec_own = vec_part[:, seg : 2 * seg]

    def vpart_copy(way):
        return pltpu.make_async_remote_copy(
            src_ref=vpart_send.at[way],
            dst_ref=vpart_recv.at[way],
            send_sem=vpart_sems.at[way, 0],
            recv_sem=vpart_sems.at[way, 1],
            device_id=along(2 * way - 1),
            device_id_type=MESH,
        )

    def part_copy(way, e):
        return pltpu.make_async_remote_copy(
            src_ref=part_send.at[way, e],
            dst_ref=part_recv.at[way, e],
            send_sem=part_sems.at[way, e, 0],
            recv_sem=part_sems.at[way, e, 1],
            device_id=along(2 * way - 1),
            device_id_type=MESH,
        )

    sends_to = (has_below, has_above)
    gets_from = (has_above, has_below)

    def start(copy, way):
        @pl.when(sends_to[way])
        def _():
            copy.start()

    def wait_recv(copy, way):
        @pl.when(gets_from[way])
        def _():
            copy.wait_recv()

    def wait_send(copy, way):
        @pl.when(sends_to[way])
        def _():
            copy.wait_send()

    for way in range(2):
        start(vpart_copy(way), way)

    a_lane = lax.broadcasted_iota(jnp.int32, (1, ka * width), 1)

    def columns_of(f):
        cols = [a_cols[f, k] for k in range(ka)]
        row = jnp.where(a_lane < width, cols[0], cols[1])
        for k in range(2, ka):
            row = jnp.where(a_lane >= k * width, cols[k], row)
        return cols, row

    def at_row(f):
        return pl.ds(pl.multiple_of(f * width, width), width)

    def near_body(i, carry):
        for t in range(UNROLL):
            f = i * UNROLL + t
            cols, row = columns_of(f)
            keep = jnp.where(row < nf, 1.0, 0.0).astype(BF16)
            table = jnp.concatenate([own[jnp.where(x < nf, x, 0)] for x in cols], axis=0)
            product = jnp.dot(a_ref[f] * keep, table, preferred_element_type=F32)
            appl[1, at_row(f), :] = product.astype(BF16)
        return carry

    lax.fori_loop(0, nf // UNROLL, near_body, 0)

    def restricted(side, e):
        return jnp.dot(
            rd[side * seg : (side + 1) * seg, :], appl[e], preferred_element_type=F32
        )

    def send_part(way, e):
        part_send[way, e] = restricted(2 * way, e).astype(BF16)
        start(part_copy(way, e), way)

    send_part(0, 1)
    send_part(1, 1)
    own_part[1] = restricted(1, 1)

    @pl.when(has_below)
    def _():
        ghost_up.wait_recv()

    @pl.when(has_above)
    def _():
        ghost_down.wait_recv()

    def far_body(i, carry):
        for t in range(UNROLL):
            f = i * UNROLL + t
            cols, row = columns_of(f)
            a_row = a_ref[f]
            low = jnp.where((row >= nf) & (row < nf + gh), 1.0, 0.0).astype(BF16)
            high = jnp.where(row >= nf + gh, 1.0, 0.0).astype(BF16)
            both = jnp.concatenate([a_row * low, a_row * high], axis=0)
            table = jnp.concatenate([ghost[jnp.where(x < nf, 0, x - nf)] for x in cols], axis=0)
            product = jnp.dot(both, table, preferred_element_type=F32).astype(BF16)
            appl[0, at_row(f), :] = product[:width]
            appl[2, at_row(f), :] = product[width:]
        return carry

    lax.fori_loop(0, nf // UNROLL, far_body, 0)
    send_part(1, 0)
    send_part(0, 2)
    send_part(1, 2)
    send_part(0, 0)
    own_part[0] = restricted(1, 0)
    own_part[2] = restricted(1, 2)

    owners = [dest[s, 0] for s in range(nc)]
    ranks = []
    for s in range(nc):
        rank = jnp.int32(0)
        for before in range(s):
            rank = rank + jnp.where(owners[before] == owners[s], 1, 0)
        ranks.append(rank)
    sources = []
    for r in range(comp_count):
        to = lax.rem(c + r, comp_count)
        for k in range(cap):
            source = jnp.int32(nc)
            for s in range(nc):
                source = jnp.where((owners[s] == to) & (ranks[s] == k), s, source)
            sources.append(source)

    own_rows = pl.ds(c * cap, cap)

    def slot_copy(u, r):
        return pltpu.make_async_remote_copy(
            src_ref=slots.at[u, r],
            dst_ref=out_ref.at[own_rows, :, pl.ds(u * seg, seg)],
            send_sem=slot_sems.at[u, r - 1, 0],
            recv_sem=slot_sems.at[u, r - 1, 1],
            device_id=peer(r),
            device_id_type=MESH,
        )

    def local_copy(u):
        return pltpu.make_async_copy(
            slots.at[u, 0], out_ref.at[own_rows, :, pl.ds(u * seg, seg)], local_sems.at[u]
        )

    def finish(u):
        total = None
        if 1 <= u <= 3:
            total = own_part[u - 1]
        if u >= 2:
            term = part_recv[0, u - 2].astype(F32)
            total = term if total is None else total + term
        if u <= 2:
            term = part_recv[1, u].astype(F32)
            total = term if total is None else total + term
        rounded = total.astype(BF16)
        for s in range(nc):
            rows[u, s] = rounded[s * width : (s + 1) * width]
        rows[u, nc] = jnp.zeros((width, seg), BF16)
        for r in range(1, comp_count):
            for k in range(cap):
                slots[u, r, k] = rows[u, sources[r * cap + k]]
            slot_copy(u, r).start()
        for k in range(cap):
            slots[u, 0, k] = rows[u, sources[k]]
        local_copy(u).start()

    for way in range(2):
        wait_recv(vpart_copy(way), way)
    vec_total = vec_own + vpart_recv[0] + vpart_recv[1]
    vrows[...] = jnp.zeros_like(vrows)
    for s in range(nc):
        cut = slice(s * width, (s + 1) * width)
        both = jnp.concatenate([vec_total[0:1, cut], vec_total[1:2, cut]], axis=1)
        vrows[s, 0:1, :] = both
    for r in range(comp_count):
        picked = [vrows[sources[r * cap + k]] for k in range(cap)]
        for k in range(cap):
            vslots[r, k] = picked[k]

    def vslot_copy(r):
        return pltpu.make_async_remote_copy(
            src_ref=vslots.at[r],
            dst_ref=vslots_recv.at[r],
            send_sem=vslot_sems.at[r - 1, 0],
            recv_sem=vslot_sems.at[r - 1, 1],
            device_id=peer(r),
            device_id_type=MESH,
        )

    for r in range(1, comp_count):
        vslot_copy(r).start()

    wait_recv(part_copy(1, 1), 1)
    finish(1)
    wait_recv(part_copy(0, 1), 0)
    finish(3)
    wait_recv(part_copy(1, 0), 1)
    finish(0)
    wait_recv(part_copy(0, 2), 0)
    finish(4)
    wait_recv(part_copy(1, 2), 1)
    wait_recv(part_copy(0, 0), 0)
    finish(2)

    vslots_recv[0] = vslots[0]
    for r in range(1, comp_count):
        vslot_copy(r).wait_recv()
    for x in range(comp_count):
        for k in range(cap):
            row = jnp.zeros((1, 2 * width), F32)
            for r in range(comp_count):
                from_x = lax.rem(c + comp_count - r, comp_count) == x
                row = row + jnp.where(from_x, 1.0, 0.0) * vslots_recv[r, k, 0:1, :]
            out_vec[x * cap + k : x * cap + k + 1, :] = row

    for u in range(5):
        for r in range(1, comp_count):
            slot_copy(u, r).wait_recv()
        local_copy(u).wait()
    for r in range(1, comp_count):
        vslot_copy(r).wait_send()
        for u in range(5):
            slot_copy(u, r).wait_send()
    for way in range(2):
        wait_send(vpart_copy(way), way)
        for e in range(3):
            wait_send(part_copy(way, e), way)

    @pl.when(has_above)
    def _():
        ghost_up.wait_send()

    @pl.when(has_below)
    def _():
        ghost_down.wait_send()


def on_device(
    mesh_count,
    comp_count,
    a_blocks,
    a_columns,
    p_blocks,
    p_columns,
    r_blocks,
    r_columns,
    sent_up,
    sent_down,
    vectors,
    coarse_dest,
):
    nf, width = a_blocks.shape[:2]
    ka, kp, kr = a_columns.shape[1], p_columns.shape[1], r_columns.shape[1]
    gh, nc = sent_up.shape[0], coarse_dest.shape[0]
    cap = max(2, nc // 2)
    seg = nc * width
    sizes = (mesh_count, comp_count, nf, width, ka, kp, kr, gh, nc, cap)
    smem = pl.BlockSpec(memory_space=pltpu.SMEM)
    vmem = pl.BlockSpec(memory_space=pltpu.VMEM)
    matrix, vecs = pl.pallas_call(
        functools.partial(kernel, sizes),
        out_shape=(
            jax.ShapeDtypeStruct((comp_count * cap, width, 5 * seg), BF16),
            jax.ShapeDtypeStruct((comp_count * cap, 2 * width), F32),
        ),
        in_specs=[smem] * 6 + [vmem] * 4,
        out_specs=(pl.BlockSpec(memory_space=pl.ANY), vmem),
        scratch_shapes=[
            pltpu.VMEM((width, seg), BF16),
            pltpu.VMEM((nf, width, seg), BF16),
            pltpu.VMEM((2 * gh, width, seg), BF16),
            pltpu.VMEM((2 * gh, width, seg), BF16),
            pltpu.VMEM((3 * seg, nf * width), BF16),
            pltpu.VMEM((3, nf * width, seg), BF16),
            pltpu.VMEM((2, 3, seg, seg), BF16),
            pltpu.VMEM((2, 3, seg, seg), BF16),
            pltpu.VMEM((3, seg, seg), F32),
            pltpu.VMEM((5, nc + 1, width, seg), BF16),
            pltpu.VMEM((5, comp_count, cap, width, seg), BF16),
            pltpu.VMEM((nf, 2 * width), F32),
            pltpu.VMEM((8, nf * width), F32),
            pltpu.VMEM((2, 8, seg), F32),
            pltpu.VMEM((2, 8, seg), F32),
            pltpu.VMEM((nc + 1, 8, 2 * width), F32),
            pltpu.VMEM((comp_count, cap, 8, 2 * width), F32),
            pltpu.VMEM((comp_count, cap, 8, 2 * width), F32),
            pltpu.SemaphoreType.DMA((4,)),
            pltpu.SemaphoreType.DMA((2, 3, 2)),
            pltpu.SemaphoreType.DMA((2, 2)),
            pltpu.SemaphoreType.DMA((5, comp_count - 1, 2)),
            pltpu.SemaphoreType.DMA((5,)),
            pltpu.SemaphoreType.DMA((comp_count - 1, 2)),
        ],
        compiler_params=pltpu.CompilerParams(
            collective_id=0, has_side_effects=True, vmem_limit_bytes=48 * 1024 * 1024
        ),
    )(
        a_columns,
        p_columns,
        r_columns,
        sent_up,
        sent_down,
        coarse_dest,
        a_blocks,
        p_blocks,
        r_blocks,
        vectors,
    )
    return matrix, vecs.astype(BF16)


def solution(mesh):
    placed = (
        P(("mesh", "comp"), None, None),
        P(("mesh", "comp"), None),
        P(("mesh", "comp"), None, None),
        P(("mesh", "comp"), None),
        P(("mesh", "comp"), None, None),
        P(("mesh", "comp"), None),
        P(("mesh", "comp")),
        P(("mesh", "comp")),
        P(("mesh", "comp"), None),
        P(("mesh", "comp"), None),
    )
    return jax.shard_map(
        functools.partial(on_device, mesh.shape["mesh"], mesh.shape["comp"]),
        mesh=mesh,
        in_specs=placed,
        out_specs=(P(("mesh", "comp"), None, None), P(("mesh", "comp"), None)),
        check_vma=False,
    )
```

```python
import functools

import jax
import jax.numpy as jnp
from jax import lax
from jax.experimental import pallas as pl
from jax.experimental.pallas import tpu as pltpu
from jax.sharding import PartitionSpec as P

MESH = pl.DeviceIdType.MESH
F32 = jnp.float32
BF16 = jnp.bfloat16
UNROLL = 4
WIDE = 8


def kernel(
    sizes,
    a_cols,
    p_cols,
    r_cols,
    up_rows,
    down_rows,
    dest,
    a_hbm,
    p_hbm,
    r_hbm,
    vec_hbm,
    out_ref,
    out_vec,
    a_ref,
    p_ref,
    r_ref,
    vec_ref,
    own,
    ghost,
    ghost_send,
    rd,
    appl,
    part_send,
    part_recv,
    own_part,
    rows,
    slots,
    vec_f32,
    vec_t,
    vpart_send,
    vpart_recv,
    vrows,
    vslots,
    vslots_recv,
    ghost_sems,
    part_sems,
    vpart_sems,
    slot_sems,
    local_sems,
    vslot_sems,
    in_sems,
):
    mesh_count, comp_count, nf, width, ka, kp, kr, gh, nc, cap = sizes
    seg = nc * width
    m = lax.axis_index("mesh")
    c = lax.axis_index("comp")
    has_below = m > 0
    has_above = m < mesh_count - 1

    def along(step):
        return (m + step, c)

    def peer(r):
        return (m, lax.rem(c + r, comp_count))

    inputs = [
        pltpu.make_async_copy(source, target, in_sems.at[i])
        for i, (source, target) in enumerate(
            ((p_hbm, p_ref), (r_hbm, r_ref), (vec_hbm, vec_ref), (a_hbm, a_ref))
        )
    ]
    for copy in inputs:
        copy.start()

    ghost[...] = jnp.zeros_like(ghost)
    part_recv[...] = jnp.zeros_like(part_recv)
    vpart_recv[...] = jnp.zeros_like(vpart_recv)

    barrier = pltpu.get_barrier_semaphore()
    for r in range(1, comp_count):
        pl.semaphore_signal(barrier, inc=1, device_id=peer(r), device_id_type=MESH)

    @pl.when(has_above)
    def _():
        pl.semaphore_signal(barrier, inc=1, device_id=along(1), device_id_type=MESH)

    @pl.when(has_below)
    def _():
        pl.semaphore_signal(barrier, inc=1, device_id=along(-1), device_id_type=MESH)

    pair_lane = lax.broadcasted_iota(jnp.int32, (1, 2 * width), 1)
    first_half = pair_lane < width

    def dense_row(f):
        strip = p_ref[f]
        blocks = []
        for q in range(kp):
            block = strip[:, q * width : (q + 1) * width]
            blocks.append(jnp.concatenate([block, block], axis=1))
        tiles = []
        for s in range(0, nc, 2):
            here = jnp.where(first_half, s, s + 1)
            total = None
            for q in range(kp):
                term = blocks[q] * jnp.where(here == p_cols[q, f], 1.0, 0.0).astype(BF16)
                total = term if total is None else total + term
            tiles.append(total)
        return jnp.concatenate(tiles, axis=1)

    def fill_ghosts(listed, at):
        def body(i, carry):
            for t in range(UNROLL):
                g = i * UNROLL + t
                ghost_send[at + g] = dense_row(listed[g])
            return carry

        lax.fori_loop(0, gh // UNROLL, body, 0)

    ghost_up = pltpu.make_async_remote_copy(
        src_ref=ghost_send.at[pl.ds(0, gh)],
        dst_ref=ghost.at[pl.ds(0, gh)],
        send_sem=ghost_sems.at[0],
        recv_sem=ghost_sems.at[1],
        device_id=along(1),
        device_id_type=MESH,
    )
    ghost_down = pltpu.make_async_remote_copy(
        src_ref=ghost_send.at[pl.ds(gh, gh)],
        dst_ref=ghost.at[pl.ds(gh, gh)],
        send_sem=ghost_sems.at[2],
        recv_sem=ghost_sems.at[3],
        device_id=along(-1),
        device_id_type=MESH,
    )
    inputs[0].wait()
    fill_ghosts(up_rows, 0)
    pl.semaphore_wait(
        barrier,
        comp_count - 1 + jnp.where(has_below, 1, 0) + jnp.where(has_above, 1, 0),
    )

    @pl.when(has_above)
    def _():
        ghost_up.start()

    fill_ghosts(down_rows, gh)

    @pl.when(has_below)
    def _():
        ghost_down.start()

    def own_body(i, carry):
        for t in range(UNROLL):
            f = i * UNROLL + t
            own[f] = dense_row(f)
        return carry

    lax.fori_loop(0, nf // UNROLL, own_body, 0)

    inputs[1].wait()
    inputs[2].wait()
    vec_f32[...] = vec_ref[...].astype(F32)
    vec_t[...] = jnp.zeros_like(vec_t)
    def rd_body(i, carry):
        f = i * 2
        at = pl.ds(pl.multiple_of(i * 2 * width, 2 * width), 2 * width)
        even = r_ref[f]
        odd = r_ref[f + 1]
        blocks = []
        named = []
        for j in range(kr):
            cut = slice(j * width, (j + 1) * width)
            blocks.append(jnp.concatenate([even[:, cut], odd[:, cut]], axis=1))
            named.append(jnp.where(first_half, r_cols[j, f], r_cols[j, f + 1]))
        for target in range(3 * nc):
            total = None
            for j in range(kr):
                hit = jnp.where(named[j] == target, 1.0, 0.0).astype(BF16)
                term = blocks[j] * hit
                total = term if total is None else total + term
            rd[target * width : (target + 1) * width, at] = total
        v0 = vec_f32[pl.ds(f, 1), :]
        v1 = vec_f32[pl.ds(f + 1, 1), :]
        vec_t[0:1, at] = jnp.where(first_half, v0, pltpu.roll(v1, width, 1))
        vec_t[1:2, at] = jnp.where(first_half, pltpu.roll(v0, width, 1), v1)
        return carry

    lax.fori_loop(0, nf // 2, rd_body, 0)

    vec_part = lax.dot_general(
        vec_t[...].astype(BF16),
        rd[...],
        (((1,), (1,)), ((), ())),
        preferred_element_type=F32,
    )
    vpart_send[0] = vec_part[:, 0:seg]
    vpart_send[1] = vec_part[:, 2 * seg : 3 * seg]
    vec_own = vec_part[:, seg : 2 * seg]

    def vpart_copy(way):
        return pltpu.make_async_remote_copy(
            src_ref=vpart_send.at[way],
            dst_ref=vpart_recv.at[way],
            send_sem=vpart_sems.at[way, 0],
            recv_sem=vpart_sems.at[way, 1],
            device_id=along(2 * way - 1),
            device_id_type=MESH,
        )

    def part_copy(way, e):
        return pltpu.make_async_remote_copy(
            src_ref=part_send.at[way, e],
            dst_ref=part_recv.at[way, e],
            send_sem=part_sems.at[way, e, 0],
            recv_sem=part_sems.at[way, e, 1],
            device_id=along(2 * way - 1),
            device_id_type=MESH,
        )

    sends_to = (has_below, has_above)
    gets_from = (has_above, has_below)

    def start(copy, way):
        @pl.when(sends_to[way])
        def _():
            copy.start()

    def wait_recv(copy, way):
        @pl.when(gets_from[way])
        def _():
            copy.wait_recv()

    def wait_send(copy, way):
        @pl.when(sends_to[way])
        def _():
            copy.wait_send()

    for way in range(2):
        start(vpart_copy(way), way)

    a_lane = lax.broadcasted_iota(jnp.int32, (1, ka * width), 1)

    def columns_of(f):
        cols = [a_cols[k, f] for k in range(ka)]
        row = jnp.where(a_lane < width, cols[0], cols[1])
        for k in range(2, ka):
            row = jnp.where(a_lane >= k * width, cols[k], row)
        return cols, row

    def at_row(f):
        return pl.ds(pl.multiple_of(f * width, width), width)

    def near_body(i, carry):
        for t in range(WIDE):
            f = i * WIDE + t
            cols, row = columns_of(f)
            keep = jnp.where(row < nf, 1.0, 0.0).astype(BF16)
            table = jnp.concatenate([own[jnp.where(x < nf, x, 0)] for x in cols], axis=0)
            product = jnp.dot(a_ref[f] * keep, table, preferred_element_type=F32)
            appl[1, at_row(f), :] = product.astype(BF16)
        return carry

    inputs[3].wait()
    lax.fori_loop(0, nf // WIDE, near_body, 0)

    def restrict(e):
        terms = jnp.dot(rd[...], appl[e], preferred_element_type=F32)
        part_send[0, e] = terms[:seg].astype(BF16)
        own_part[e] = terms[seg : 2 * seg]
        part_send[1, e] = terms[2 * seg :].astype(BF16)

    restrict(1)
    for way in range(2):
        start(part_copy(way, 1), way)

    @pl.when(has_below)
    def _():
        ghost_up.wait_recv()

    @pl.when(has_above)
    def _():
        ghost_down.wait_recv()

    def far_body(i, carry):
        for t in range(WIDE):
            f = i * WIDE + t
            cols, row = columns_of(f)
            a_row = a_ref[f]
            low = jnp.where((row >= nf) & (row < nf + gh), 1.0, 0.0).astype(BF16)
            high = jnp.where(row >= nf + gh, 1.0, 0.0).astype(BF16)
            both = jnp.concatenate([a_row * low, a_row * high], axis=0)
            table = jnp.concatenate([ghost[jnp.where(x < nf, 0, x - nf)] for x in cols], axis=0)
            product = jnp.dot(both, table, preferred_element_type=F32).astype(BF16)
            appl[0, at_row(f), :] = product[:width]
            appl[2, at_row(f), :] = product[width:]
        return carry

    lax.fori_loop(0, nf // WIDE, far_body, 0)
    restrict(0)
    start(part_copy(1, 0), 1)
    restrict(2)
    start(part_copy(0, 2), 0)
    start(part_copy(1, 2), 1)
    start(part_copy(0, 0), 0)

    owners = [dest[s] for s in range(nc)]
    ranks = []
    for s in range(nc):
        rank = jnp.int32(0)
        for before in range(s):
            rank = rank + jnp.where(owners[before] == owners[s], 1, 0)
        ranks.append(rank)
    sources = []
    for r in range(comp_count):
        to = lax.rem(c + r, comp_count)
        for k in range(cap):
            source = jnp.int32(nc)
            for s in range(nc):
                source = jnp.where((owners[s] == to) & (ranks[s] == k), s, source)
            sources.append(source)

    own_rows = pl.ds(c * cap, cap)

    def slot_copy(u, r):
        return pltpu.make_async_remote_copy(
            src_ref=slots.at[u, r],
            dst_ref=out_ref.at[own_rows, :, pl.ds(u * seg, seg)],
            send_sem=slot_sems.at[u, r - 1, 0],
            recv_sem=slot_sems.at[u, r - 1, 1],
            device_id=peer(r),
            device_id_type=MESH,
        )

    def local_copy(u):
        return pltpu.make_async_copy(
            slots.at[u, 0], out_ref.at[own_rows, :, pl.ds(u * seg, seg)], local_sems.at[u]
        )

    def finish(u):
        total = None
        if 1 <= u <= 3:
            total = own_part[u - 1]
        if u >= 2:
            term = part_recv[0, u - 2].astype(F32)
            total = term if total is None else total + term
        if u <= 2:
            term = part_recv[1, u].astype(F32)
            total = term if total is None else total + term
        rounded = total.astype(BF16)
        for s in range(nc):
            rows[u, s] = rounded[s * width : (s + 1) * width]
        rows[u, nc] = jnp.zeros((width, seg), BF16)
        for r in range(1, comp_count):
            for k in range(cap):
                slots[u, r, k] = rows[u, sources[r * cap + k]]
            slot_copy(u, r).start()
        for k in range(cap):
            slots[u, 0, k] = rows[u, sources[k]]
        local_copy(u).start()

    for way in range(2):
        wait_recv(vpart_copy(way), way)
    vec_total = vec_own + vpart_recv[0] + vpart_recv[1]
    vrows[...] = jnp.zeros_like(vrows)
    for s in range(nc):
        cut = slice(s * width, (s + 1) * width)
        both = jnp.concatenate([vec_total[0:1, cut], vec_total[1:2, cut]], axis=1)
        vrows[s, 0:1, :] = both
    for r in range(comp_count):
        picked = [vrows[sources[r * cap + k]] for k in range(cap)]
        for k in range(cap):
            vslots[r, k] = picked[k]

    def vslot_copy(r):
        return pltpu.make_async_remote_copy(
            src_ref=vslots.at[r],
            dst_ref=vslots_recv.at[r],
            send_sem=vslot_sems.at[r - 1, 0],
            recv_sem=vslot_sems.at[r - 1, 1],
            device_id=peer(r),
            device_id_type=MESH,
        )

    for r in range(1, comp_count):
        vslot_copy(r).start()

    wait_recv(part_copy(1, 1), 1)
    finish(1)
    wait_recv(part_copy(0, 1), 0)
    finish(3)
    wait_recv(part_copy(1, 0), 1)
    finish(0)
    wait_recv(part_copy(0, 2), 0)
    finish(4)
    wait_recv(part_copy(1, 2), 1)
    wait_recv(part_copy(0, 0), 0)
    finish(2)

    vslots_recv[0] = vslots[0]
    for r in range(1, comp_count):
        vslot_copy(r).wait_recv()
    vec_rows = []
    for x in range(comp_count):
        for k in range(cap):
            row = jnp.zeros((1, 2 * width), F32)
            for r in range(comp_count):
                from_x = lax.rem(c + comp_count - r, comp_count) == x
                row = row + jnp.where(from_x, 1.0, 0.0) * vslots_recv[r, k, 0:1, :]
            vec_rows.append(row)
    out_vec[...] = jnp.concatenate(vec_rows, axis=0).astype(BF16)

    for u in range(5):
        for r in range(1, comp_count):
            slot_copy(u, r).wait_recv()
        local_copy(u).wait()
    for r in range(1, comp_count):
        vslot_copy(r).wait_send()
        for u in range(5):
            slot_copy(u, r).wait_send()
    for way in range(2):
        wait_send(vpart_copy(way), way)
        for e in range(3):
            wait_send(part_copy(way, e), way)

    @pl.when(has_above)
    def _():
        ghost_up.wait_send()

    @pl.when(has_below)
    def _():
        ghost_down.wait_send()


def on_device(
    mesh_count,
    comp_count,
    a_blocks,
    a_columns,
    p_blocks,
    p_columns,
    r_blocks,
    r_columns,
    sent_up,
    sent_down,
    vectors,
    coarse_dest,
):
    nf, width = a_blocks.shape[:2]
    ka, kp, kr = a_columns.shape[1], p_columns.shape[1], r_columns.shape[1]
    gh, nc = sent_up.shape[0], coarse_dest.shape[0]
    cap = max(2, nc // 2)
    seg = nc * width
    sizes = (mesh_count, comp_count, nf, width, ka, kp, kr, gh, nc, cap)
    smem = pl.BlockSpec(memory_space=pltpu.SMEM)
    hbm = pl.BlockSpec(memory_space=pl.ANY)
    vmem = pl.BlockSpec(memory_space=pltpu.VMEM)
    return pl.pallas_call(
        functools.partial(kernel, sizes),
        out_shape=(
            jax.ShapeDtypeStruct((comp_count * cap, width, 5 * seg), BF16),
            jax.ShapeDtypeStruct((comp_count * cap, 2 * width), BF16),
        ),
        in_specs=[smem] * 6 + [hbm] * 4,
        out_specs=(hbm, vmem),
        scratch_shapes=[
            pltpu.VMEM(a_blocks.shape, BF16),
            pltpu.VMEM(p_blocks.shape, BF16),
            pltpu.VMEM(r_blocks.shape, BF16),
            pltpu.VMEM(vectors.shape, BF16),
            pltpu.VMEM((nf, width, seg), BF16),
            pltpu.VMEM((2 * gh, width, seg), BF16),
            pltpu.VMEM((2 * gh, width, seg), BF16),
            pltpu.VMEM((3 * seg, nf * width), BF16),
            pltpu.VMEM((3, nf * width, seg), BF16),
            pltpu.VMEM((2, 3, seg, seg), BF16),
            pltpu.VMEM((2, 3, seg, seg), BF16),
            pltpu.VMEM((3, seg, seg), F32),
            pltpu.VMEM((5, nc + 1, width, seg), BF16),
            pltpu.VMEM((5, comp_count, cap, width, seg), BF16),
            pltpu.VMEM((nf, 2 * width), F32),
            pltpu.VMEM((8, nf * width), F32),
            pltpu.VMEM((2, 8, seg), F32),
            pltpu.VMEM((2, 8, seg), F32),
            pltpu.VMEM((nc + 1, 8, 2 * width), F32),
            pltpu.VMEM((comp_count, cap, 8, 2 * width), F32),
            pltpu.VMEM((comp_count, cap, 8, 2 * width), F32),
            pltpu.SemaphoreType.DMA((4,)),
            pltpu.SemaphoreType.DMA((2, 3, 2)),
            pltpu.SemaphoreType.DMA((2, 2)),
            pltpu.SemaphoreType.DMA((5, comp_count - 1, 2)),
            pltpu.SemaphoreType.DMA((5,)),
            pltpu.SemaphoreType.DMA((comp_count - 1, 2)),
            pltpu.SemaphoreType.DMA((4,)),
        ],
        compiler_params=pltpu.CompilerParams(
            collective_id=0, has_side_effects=True, vmem_limit_bytes=60 * 1024 * 1024
        ),
    )(
        a_columns.T,
        p_columns.T,
        r_columns.T,
        sent_up,
        sent_down,
        coarse_dest.reshape(nc),
        a_blocks,
        p_blocks,
        r_blocks,
        vectors,
    )


def solution(mesh):
    placed = (
        P(("mesh", "comp"), None, None),
        P(("mesh", "comp"), None),
        P(("mesh", "comp"), None, None),
        P(("mesh", "comp"), None),
        P(("mesh", "comp"), None, None),
        P(("mesh", "comp"), None),
        P(("mesh", "comp")),
        P(("mesh", "comp")),
        P(("mesh", "comp"), None),
        P(("mesh", "comp"), None),
    )
    return jax.shard_map(
        functools.partial(on_device, mesh.shape["mesh"], mesh.shape["comp"]),
        mesh=mesh,
        in_specs=placed,
        out_specs=(P(("mesh", "comp"), None, None), P(("mesh", "comp"), None)),
        check_vma=False,
    )
```

```python
import functools

import jax
import jax.numpy as jnp
from jax import lax
from jax.experimental import pallas as pl
from jax.experimental.pallas import tpu as pltpu
from jax.sharding import PartitionSpec as P

MESH = pl.DeviceIdType.MESH
F32 = jnp.float32
BF16 = jnp.bfloat16
UNROLL = 4
WIDE = 8


def kernel(
    sizes,
    a_cols,
    p_cols,
    r_cols,
    up_rows,
    down_rows,
    dest,
    a_hbm,
    p_hbm,
    r_hbm,
    vec_hbm,
    out_ref,
    out_vec,
    a_ref,
    p_ref,
    r_ref,
    vec_ref,
    own,
    ghost,
    raw_send,
    raw_recv,
    name_send,
    name_recv,
    rd,
    appl,
    part_send,
    part_recv,
    own_part,
    rows,
    slots,
    vec_f32,
    vec_t,
    vpart_send,
    vpart_recv,
    vrows,
    vslots,
    vslots_recv,
    ghost_sems,
    part_sems,
    vpart_sems,
    slot_sems,
    local_sems,
    vslot_sems,
    in_sems,
):
    mesh_count, comp_count, nf, width, ka, kp, kr, gh, nc, cap = sizes
    seg = nc * width
    m = lax.axis_index("mesh")
    c = lax.axis_index("comp")
    has_below = m > 0
    has_above = m < mesh_count - 1

    def along(step):
        return (m + step, c)

    def peer(r):
        return (m, lax.rem(c + r, comp_count))

    inputs = [
        pltpu.make_async_copy(source, target, in_sems.at[i])
        for i, (source, target) in enumerate(
            ((p_hbm, p_ref), (r_hbm, r_ref), (vec_hbm, vec_ref), (a_hbm, a_ref))
        )
    ]
    for copy in inputs:
        copy.start()

    raw_recv[...] = jnp.zeros_like(raw_recv)
    name_recv[...] = jnp.zeros_like(name_recv)
    part_recv[...] = jnp.zeros_like(part_recv)
    vpart_recv[...] = jnp.zeros_like(vpart_recv)

    barrier = pltpu.get_barrier_semaphore()
    for r in range(1, comp_count):
        pl.semaphore_signal(barrier, inc=1, device_id=peer(r), device_id_type=MESH)

    @pl.when(has_above)
    def _():
        pl.semaphore_signal(barrier, inc=1, device_id=along(1), device_id_type=MESH)

    @pl.when(has_below)
    def _():
        pl.semaphore_signal(barrier, inc=1, device_id=along(-1), device_id_type=MESH)

    pair_lane = lax.broadcasted_iota(jnp.int32, (1, 2 * width), 1)
    first_half = pair_lane < width

    def twice(block):
        return jnp.concatenate([block, block], axis=1)

    def spread(blocks, names):
        tiles = []
        for s in range(0, nc, 2):
            here = jnp.where(first_half, s, s + 1).astype(F32)
            total = None
            for block, name in zip(blocks, names):
                term = block * jnp.where(here == name, 1.0, 0.0).astype(BF16)
                total = term if total is None else total + term
            tiles.append(total)
        return jnp.concatenate(tiles, axis=1)

    def dense_row(f):
        strip = p_ref[f]
        blocks = [twice(strip[:, q * width : (q + 1) * width]) for q in range(kp)]
        return spread(blocks, [p_cols[q, f].astype(F32) for q in range(kp)])

    def fill_ghosts(way, listed):
        def body(i, carry):
            rows_of = [listed[2 * i], listed[2 * i + 1]]
            strips = [p_ref[f] for f in rows_of]
            raw_send[way, i, 0] = strips[0][:, : 2 * width]
            raw_send[way, i, 1] = strips[1][:, : 2 * width]
            raw_send[way, i, 2] = jnp.concatenate([x[:, 2 * width :] for x in strips], axis=1)
            names = [
                jnp.zeros((1, 2 * width), F32) + p_cols[q, f].astype(F32)
                for f in rows_of
                for q in range(kp)
            ]
            names.append(jnp.zeros((8 - 2 * kp, 2 * width), F32))
            name_send[way, i] = jnp.concatenate(names, axis=0)
            return carry

        lax.fori_loop(0, gh // 2, body, 0)

    def ghost_copies(way):
        return [
            pltpu.make_async_remote_copy(
                src_ref=source.at[way],
                dst_ref=target.at[way],
                send_sem=ghost_sems.at[way, i, 0],
                recv_sem=ghost_sems.at[way, i, 1],
                device_id=along(2 * way - 1),
                device_id_type=MESH,
            )
            for i, (source, target) in enumerate(((raw_send, raw_recv), (name_send, name_recv)))
        ]

    def arrived_ghosts(way, at):
        def body(i, carry):
            last = raw_recv[way, i, 2]
            for t in range(2):
                pair = raw_recv[way, i, t]
                blocks = [
                    twice(pair[:, :width]),
                    twice(pair[:, width:]),
                    twice(last[:, t * width : (t + 1) * width]),
                ]
                names = [name_recv[way, i, t * kp + q : t * kp + q + 1, :] for q in range(kp)]
                ghost[at + 2 * i + t] = spread(blocks, names)
            return carry

        lax.fori_loop(0, gh // 2, body, 0)

    inputs[0].wait()
    fill_ghosts(1, up_rows)
    pl.semaphore_wait(
        barrier,
        comp_count - 1 + jnp.where(has_below, 1, 0) + jnp.where(has_above, 1, 0),
    )

    @pl.when(has_above)
    def _():
        for copy in ghost_copies(1):
            copy.start()

    fill_ghosts(0, down_rows)

    @pl.when(has_below)
    def _():
        for copy in ghost_copies(0):
            copy.start()

    def own_body(i, carry):
        for t in range(UNROLL):
            f = i * UNROLL + t
            own[f] = dense_row(f)
        return carry

    lax.fori_loop(0, nf // UNROLL, own_body, 0)

    inputs[1].wait()
    inputs[2].wait()
    vec_f32[...] = vec_ref[...].astype(F32)
    vec_t[...] = jnp.zeros_like(vec_t)
    def rd_body(i, carry):
        f = i * 2
        at = pl.ds(pl.multiple_of(i * 2 * width, 2 * width), 2 * width)
        even = r_ref[f]
        odd = r_ref[f + 1]
        blocks = []
        named = []
        for j in range(kr):
            cut = slice(j * width, (j + 1) * width)
            blocks.append(jnp.concatenate([even[:, cut], odd[:, cut]], axis=1))
            named.append(jnp.where(first_half, r_cols[j, f], r_cols[j, f + 1]))
        for target in range(3 * nc):
            total = None
            for j in range(kr):
                hit = jnp.where(named[j] == target, 1.0, 0.0).astype(BF16)
                term = blocks[j] * hit
                total = term if total is None else total + term
            rd[target * width : (target + 1) * width, at] = total
        v0 = vec_f32[pl.ds(f, 1), :]
        v1 = vec_f32[pl.ds(f + 1, 1), :]
        vec_t[0:1, at] = jnp.where(first_half, v0, pltpu.roll(v1, width, 1))
        vec_t[1:2, at] = jnp.where(first_half, pltpu.roll(v0, width, 1), v1)
        return carry

    lax.fori_loop(0, nf // 2, rd_body, 0)

    def vpart_copy(way):
        return pltpu.make_async_remote_copy(
            src_ref=vpart_send.at[way],
            dst_ref=vpart_recv.at[way],
            send_sem=vpart_sems.at[way, 0],
            recv_sem=vpart_sems.at[way, 1],
            device_id=along(2 * way - 1),
            device_id_type=MESH,
        )

    def part_copy(way, e):
        return pltpu.make_async_remote_copy(
            src_ref=part_send.at[way, e],
            dst_ref=part_recv.at[way, e],
            send_sem=part_sems.at[way, e, 0],
            recv_sem=part_sems.at[way, e, 1],
            device_id=along(2 * way - 1),
            device_id_type=MESH,
        )

    sends_to = (has_below, has_above)
    gets_from = (has_above, has_below)

    def start(copy, way):
        @pl.when(sends_to[way])
        def _():
            copy.start()

    def wait_recv(copy, way):
        @pl.when(gets_from[way])
        def _():
            copy.wait_recv()

    def wait_send(copy, way):
        @pl.when(sends_to[way])
        def _():
            copy.wait_send()

    a_lane = lax.broadcasted_iota(jnp.int32, (1, ka * width), 1)

    def columns_of(f):
        cols = [a_cols[k, f] for k in range(ka)]
        row = jnp.where(a_lane < width, cols[0], cols[1])
        for k in range(2, ka):
            row = jnp.where(a_lane >= k * width, cols[k], row)
        return cols, row

    def at_row(f):
        return pl.ds(pl.multiple_of(f * width, width), width)

    def near_body(i, carry):
        for t in range(WIDE):
            f = i * WIDE + t
            cols, row = columns_of(f)
            keep = jnp.where(row < nf, 1.0, 0.0).astype(BF16)
            table = jnp.concatenate([own[jnp.where(x < nf, x, 0)] for x in cols], axis=0)
            product = jnp.dot(a_ref[f] * keep, table, preferred_element_type=F32)
            appl[1, at_row(f), :] = product.astype(BF16)
        return carry

    inputs[3].wait()
    lax.fori_loop(0, nf // WIDE, near_body, 0)

    def restrict(e):
        terms = jnp.dot(rd[...], appl[e], preferred_element_type=F32)
        part_send[0, e] = terms[:seg].astype(BF16)
        own_part[e] = terms[seg : 2 * seg]
        part_send[1, e] = terms[2 * seg :].astype(BF16)

    restrict(1)
    vec_part = lax.dot_general(
        vec_t[...].astype(BF16),
        rd[...],
        (((1,), (1,)), ((), ())),
        preferred_element_type=F32,
    )
    vpart_send[0] = vec_part[:, 0:seg]
    vpart_send[1] = vec_part[:, 2 * seg : 3 * seg]
    vec_own = vec_part[:, seg : 2 * seg]
    @pl.when(has_below)
    def _():
        for copy in ghost_copies(1):
            copy.wait_recv()

    @pl.when(has_above)
    def _():
        for copy in ghost_copies(0):
            copy.wait_recv()

    for way in range(2):
        start(part_copy(way, 1), way)
    for way in range(2):
        start(vpart_copy(way), way)
    arrived_ghosts(1, 0)
    arrived_ghosts(0, gh)

    def far_body(i, carry):
        for t in range(WIDE):
            f = i * WIDE + t
            cols, row = columns_of(f)
            a_row = a_ref[f]
            low = jnp.where((row >= nf) & (row < nf + gh), 1.0, 0.0).astype(BF16)
            high = jnp.where(row >= nf + gh, 1.0, 0.0).astype(BF16)
            both = jnp.concatenate([a_row * low, a_row * high], axis=0)
            table = jnp.concatenate([ghost[jnp.where(x < nf, 0, x - nf)] for x in cols], axis=0)
            product = jnp.dot(both, table, preferred_element_type=F32).astype(BF16)
            appl[0, at_row(f), :] = product[:width]
            appl[2, at_row(f), :] = product[width:]
        return carry

    lax.fori_loop(0, nf // WIDE, far_body, 0)
    restrict(0)
    start(part_copy(1, 0), 1)
    restrict(2)
    start(part_copy(0, 2), 0)
    start(part_copy(1, 2), 1)
    start(part_copy(0, 0), 0)

    owners = [dest[s] for s in range(nc)]
    ranks = []
    for s in range(nc):
        rank = jnp.int32(0)
        for before in range(s):
            rank = rank + jnp.where(owners[before] == owners[s], 1, 0)
        ranks.append(rank)
    sources = []
    for r in range(comp_count):
        to = lax.rem(c + r, comp_count)
        for k in range(cap):
            source = jnp.int32(nc)
            for s in range(nc):
                source = jnp.where((owners[s] == to) & (ranks[s] == k), s, source)
            sources.append(source)

    own_rows = pl.ds(c * cap, cap)

    def slot_copy(u, r):
        return pltpu.make_async_remote_copy(
            src_ref=slots.at[u, r],
            dst_ref=out_ref.at[own_rows, :, pl.ds(u * seg, seg)],
            send_sem=slot_sems.at[u, r - 1, 0],
            recv_sem=slot_sems.at[u, r - 1, 1],
            device_id=peer(r),
            device_id_type=MESH,
        )

    def local_copy(u):
        return pltpu.make_async_copy(
            slots.at[u, 0], out_ref.at[own_rows, :, pl.ds(u * seg, seg)], local_sems.at[u]
        )

    def finish(u):
        total = None
        if 1 <= u <= 3:
            total = own_part[u - 1]
        if u >= 2:
            term = part_recv[0, u - 2].astype(F32)
            total = term if total is None else total + term
        if u <= 2:
            term = part_recv[1, u].astype(F32)
            total = term if total is None else total + term
        rounded = total.astype(BF16)
        for s in range(nc):
            rows[u, s] = rounded[s * width : (s + 1) * width]
        rows[u, nc] = jnp.zeros((width, seg), BF16)
        for r in range(1, comp_count):
            for k in range(cap):
                slots[u, r, k] = rows[u, sources[r * cap + k]]
            slot_copy(u, r).start()
        for k in range(cap):
            slots[u, 0, k] = rows[u, sources[k]]
        local_copy(u).start()

    for way in range(2):
        wait_recv(vpart_copy(way), way)
    vec_total = vec_own + vpart_recv[0] + vpart_recv[1]
    vrows[...] = jnp.zeros_like(vrows)
    for s in range(nc):
        cut = slice(s * width, (s + 1) * width)
        both = jnp.concatenate([vec_total[0:1, cut], vec_total[1:2, cut]], axis=1)
        vrows[s, 0:1, :] = both
    for r in range(comp_count):
        picked = [vrows[sources[r * cap + k]] for k in range(cap)]
        for k in range(cap):
            vslots[r, k] = picked[k]

    def vslot_copy(r):
        return pltpu.make_async_remote_copy(
            src_ref=vslots.at[r],
            dst_ref=vslots_recv.at[r],
            send_sem=vslot_sems.at[r - 1, 0],
            recv_sem=vslot_sems.at[r - 1, 1],
            device_id=peer(r),
            device_id_type=MESH,
        )

    for r in range(1, comp_count):
        vslot_copy(r).start()

    wait_recv(part_copy(1, 1), 1)
    finish(1)
    wait_recv(part_copy(0, 1), 0)
    finish(3)
    wait_recv(part_copy(1, 0), 1)
    finish(0)
    wait_recv(part_copy(0, 2), 0)
    finish(4)
    wait_recv(part_copy(1, 2), 1)
    wait_recv(part_copy(0, 0), 0)
    finish(2)

    vslots_recv[0] = vslots[0]
    for r in range(1, comp_count):
        vslot_copy(r).wait_recv()
    vec_rows = []
    for x in range(comp_count):
        for k in range(cap):
            row = jnp.zeros((1, 2 * width), F32)
            for r in range(comp_count):
                from_x = lax.rem(c + comp_count - r, comp_count) == x
                row = row + jnp.where(from_x, 1.0, 0.0) * vslots_recv[r, k, 0:1, :]
            vec_rows.append(row)
    out_vec[...] = jnp.concatenate(vec_rows, axis=0).astype(BF16)

    for u in range(5):
        for r in range(1, comp_count):
            slot_copy(u, r).wait_recv()
        local_copy(u).wait()
    for r in range(1, comp_count):
        vslot_copy(r).wait_send()
        for u in range(5):
            slot_copy(u, r).wait_send()
    for way in range(2):
        wait_send(vpart_copy(way), way)
        for e in range(3):
            wait_send(part_copy(way, e), way)

    @pl.when(has_above)
    def _():
        for copy in ghost_copies(1):
            copy.wait_send()

    @pl.when(has_below)
    def _():
        for copy in ghost_copies(0):
            copy.wait_send()


def on_device(
    mesh_count,
    comp_count,
    a_blocks,
    a_columns,
    p_blocks,
    p_columns,
    r_blocks,
    r_columns,
    sent_up,
    sent_down,
    vectors,
    coarse_dest,
):
    nf, width = a_blocks.shape[:2]
    ka, kp, kr = a_columns.shape[1], p_columns.shape[1], r_columns.shape[1]
    gh, nc = sent_up.shape[0], coarse_dest.shape[0]
    cap = max(2, nc // 2)
    seg = nc * width
    sizes = (mesh_count, comp_count, nf, width, ka, kp, kr, gh, nc, cap)
    smem = pl.BlockSpec(memory_space=pltpu.SMEM)
    hbm = pl.BlockSpec(memory_space=pl.ANY)
    vmem = pl.BlockSpec(memory_space=pltpu.VMEM)
    return pl.pallas_call(
        functools.partial(kernel, sizes),
        out_shape=(
            jax.ShapeDtypeStruct((comp_count * cap, width, 5 * seg), BF16),
            jax.ShapeDtypeStruct((comp_count * cap, 2 * width), BF16),
        ),
        in_specs=[smem] * 6 + [hbm] * 4,
        out_specs=(hbm, vmem),
        scratch_shapes=[
            pltpu.VMEM(a_blocks.shape, BF16),
            pltpu.VMEM(p_blocks.shape, BF16),
            pltpu.VMEM(r_blocks.shape, BF16),
            pltpu.VMEM(vectors.shape, BF16),
            pltpu.VMEM((nf, width, seg), BF16),
            pltpu.VMEM((2 * gh, width, seg), BF16),
            pltpu.VMEM((2, gh // 2, kp, width, 2 * width), BF16),
            pltpu.VMEM((2, gh // 2, kp, width, 2 * width), BF16),
            pltpu.VMEM((2, gh // 2, 8, 2 * width), F32),
            pltpu.VMEM((2, gh // 2, 8, 2 * width), F32),
            pltpu.VMEM((3 * seg, nf * width), BF16),
            pltpu.VMEM((3, nf * width, seg), BF16),
            pltpu.VMEM((2, 3, seg, seg), BF16),
            pltpu.VMEM((2, 3, seg, seg), BF16),
            pltpu.VMEM((3, seg, seg), F32),
            pltpu.VMEM((5, nc + 1, width, seg), BF16),
            pltpu.VMEM((5, comp_count, cap, width, seg), BF16),
            pltpu.VMEM((nf, 2 * width), F32),
            pltpu.VMEM((8, nf * width), F32),
            pltpu.VMEM((2, 8, seg), F32),
            pltpu.VMEM((2, 8, seg), F32),
            pltpu.VMEM((nc + 1, 8, 2 * width), F32),
            pltpu.VMEM((comp_count, cap, 8, 2 * width), F32),
            pltpu.VMEM((comp_count, cap, 8, 2 * width), F32),
            pltpu.SemaphoreType.DMA((2, 2, 2)),
            pltpu.SemaphoreType.DMA((2, 3, 2)),
            pltpu.SemaphoreType.DMA((2, 2)),
            pltpu.SemaphoreType.DMA((5, comp_count - 1, 2)),
            pltpu.SemaphoreType.DMA((5,)),
            pltpu.SemaphoreType.DMA((comp_count - 1, 2)),
            pltpu.SemaphoreType.DMA((4,)),
        ],
        compiler_params=pltpu.CompilerParams(
            collective_id=0, has_side_effects=True, vmem_limit_bytes=60 * 1024 * 1024
        ),
    )(
        a_columns.T,
        p_columns.T,
        r_columns.T,
        sent_up,
        sent_down,
        coarse_dest.reshape(nc),
        a_blocks,
        p_blocks,
        r_blocks,
        vectors,
    )


def solution(mesh):
    placed = (
        P(("mesh", "comp"), None, None),
        P(("mesh", "comp"), None),
        P(("mesh", "comp"), None, None),
        P(("mesh", "comp"), None),
        P(("mesh", "comp"), None, None),
        P(("mesh", "comp"), None),
        P(("mesh", "comp")),
        P(("mesh", "comp")),
        P(("mesh", "comp"), None),
        P(("mesh", "comp"), None),
    )
    return jax.shard_map(
        functools.partial(on_device, mesh.shape["mesh"], mesh.shape["comp"]),
        mesh=mesh,
        in_specs=placed,
        out_specs=(P(("mesh", "comp"), None, None), P(("mesh", "comp"), None)),
        check_vma=False,
    )
```

```python
import functools

import jax
import jax.numpy as jnp
from jax import lax
from jax.experimental import pallas as pl
from jax.experimental.pallas import tpu as pltpu
from jax.sharding import PartitionSpec as P

MESH = pl.DeviceIdType.MESH
F32 = jnp.float32
BF16 = jnp.bfloat16
UNROLL = 4
WIDE = 8


def kernel(
    sizes,
    a_cols,
    p_cols,
    r_cols,
    up_rows,
    down_rows,
    dest,
    a_hbm,
    p_hbm,
    r_hbm,
    vec_hbm,
    out_ref,
    out_vec,
    a_ref,
    p_ref,
    r_ref,
    vec_ref,
    own,
    ghost,
    raw_send,
    raw_recv,
    name_send,
    name_recv,
    rd,
    appl,
    part_send,
    part_recv,
    own_part,
    rows,
    slots,
    vec_f32,
    vec_t,
    vpart_send,
    vpart_recv,
    vrows,
    vslots,
    vslots_recv,
    ghost_sems,
    part_sems,
    vpart_sems,
    slot_sems,
    local_sems,
    vslot_sems,
    in_sems,
):
    mesh_count, comp_count, nf, width, ka, kp, kr, gh, nc, cap = sizes
    seg = nc * width
    m = lax.axis_index("mesh")
    c = lax.axis_index("comp")
    has_below = m > 0
    has_above = m < mesh_count - 1

    def along(step):
        return (m + step, c)

    def peer(r):
        return (m, lax.rem(c + r, comp_count))

    inputs = [
        pltpu.make_async_copy(source, target, in_sems.at[i])
        for i, (source, target) in enumerate(
            ((p_hbm, p_ref), (r_hbm, r_ref), (vec_hbm, vec_ref), (a_hbm, a_ref))
        )
    ]
    for copy in inputs:
        copy.start()

    raw_recv[...] = jnp.zeros_like(raw_recv)
    name_recv[...] = jnp.zeros_like(name_recv)
    part_recv[...] = jnp.zeros_like(part_recv)
    vpart_recv[...] = jnp.zeros_like(vpart_recv)

    barrier = pltpu.get_barrier_semaphore()
    for r in range(1, comp_count):
        pl.semaphore_signal(barrier, inc=1, device_id=peer(r), device_id_type=MESH)

    @pl.when(has_above)
    def _():
        pl.semaphore_signal(barrier, inc=1, device_id=along(1), device_id_type=MESH)

    @pl.when(has_below)
    def _():
        pl.semaphore_signal(barrier, inc=1, device_id=along(-1), device_id_type=MESH)

    pair_lane = lax.broadcasted_iota(jnp.int32, (1, 2 * width), 1)
    first_half = pair_lane < width

    def twice(block):
        return jnp.concatenate([block, block], axis=1)

    def spread(blocks, names):
        tiles = []
        for s in range(0, nc, 2):
            here = jnp.where(first_half, s, s + 1).astype(F32)
            total = None
            for block, name in zip(blocks, names):
                term = block * jnp.where(here == name, 1.0, 0.0).astype(BF16)
                total = term if total is None else total + term
            tiles.append(total)
        return jnp.concatenate(tiles, axis=1)

    def dense_row(f):
        strip = p_ref[f]
        blocks = [twice(strip[:, q * width : (q + 1) * width]) for q in range(kp)]
        return spread(blocks, [p_cols[q, f].astype(F32) for q in range(kp)])

    def fill_ghosts(way, listed):
        def body(i, carry):
            rows_of = [listed[2 * i], listed[2 * i + 1]]
            strips = [p_ref[f] for f in rows_of]
            raw_send[way, i, 0] = strips[0][:, : 2 * width]
            raw_send[way, i, 1] = strips[1][:, : 2 * width]
            raw_send[way, i, 2] = jnp.concatenate([x[:, 2 * width :] for x in strips], axis=1)
            names = [
                jnp.zeros((1, 2 * width), F32) + p_cols[q, f].astype(F32)
                for f in rows_of
                for q in range(kp)
            ]
            names.append(jnp.zeros((8 - 2 * kp, 2 * width), F32))
            name_send[way, i] = jnp.concatenate(names, axis=0)
            return carry

        lax.fori_loop(0, gh // 2, body, 0)

    def ghost_copies(way):
        return [
            pltpu.make_async_remote_copy(
                src_ref=source.at[way],
                dst_ref=target.at[way],
                send_sem=ghost_sems.at[way, i, 0],
                recv_sem=ghost_sems.at[way, i, 1],
                device_id=along(2 * way - 1),
                device_id_type=MESH,
            )
            for i, (source, target) in enumerate(((raw_send, raw_recv), (name_send, name_recv)))
        ]

    def arrived_ghosts(way, at):
        def body(i, carry):
            last = raw_recv[way, i, 2]
            for t in range(2):
                pair = raw_recv[way, i, t]
                blocks = [
                    twice(pair[:, :width]),
                    twice(pair[:, width:]),
                    twice(last[:, t * width : (t + 1) * width]),
                ]
                names = [name_recv[way, i, t * kp + q : t * kp + q + 1, :] for q in range(kp)]
                ghost[at + 2 * i + t] = spread(blocks, names)
            return carry

        lax.fori_loop(0, gh // 2, body, 0)

    inputs[0].wait()
    fill_ghosts(1, up_rows)
    pl.semaphore_wait(
        barrier,
        comp_count - 1 + jnp.where(has_below, 1, 0) + jnp.where(has_above, 1, 0),
    )

    @pl.when(has_above)
    def _():
        for copy in ghost_copies(1):
            copy.start()

    fill_ghosts(0, down_rows)

    @pl.when(has_below)
    def _():
        for copy in ghost_copies(0):
            copy.start()

    def own_body(i, carry):
        for t in range(UNROLL):
            f = i * UNROLL + t
            own[f] = dense_row(f)
        return carry

    lax.fori_loop(0, nf // UNROLL, own_body, 0)

    inputs[1].wait()
    inputs[2].wait()
    vec_f32[...] = vec_ref[...].astype(F32)
    vec_t[...] = jnp.zeros_like(vec_t)
    def rd_body(i, carry):
        f = i * 2
        at = pl.ds(pl.multiple_of(i * 2 * width, 2 * width), 2 * width)
        even = r_ref[f]
        odd = r_ref[f + 1]
        blocks = []
        named = []
        for j in range(kr):
            cut = slice(j * width, (j + 1) * width)
            blocks.append(jnp.concatenate([even[:, cut], odd[:, cut]], axis=1))
            named.append(jnp.where(first_half, r_cols[j, f], r_cols[j, f + 1]))
        for target in range(3 * nc):
            total = None
            for j in range(kr):
                hit = jnp.where(named[j] == target, 1.0, 0.0).astype(BF16)
                term = blocks[j] * hit
                total = term if total is None else total + term
            rd[target * width : (target + 1) * width, at] = total
        v0 = vec_f32[pl.ds(f, 1), :]
        v1 = vec_f32[pl.ds(f + 1, 1), :]
        vec_t[0:1, at] = jnp.where(first_half, v0, pltpu.roll(v1, width, 1))
        vec_t[1:2, at] = jnp.where(first_half, pltpu.roll(v0, width, 1), v1)
        return carry

    lax.fori_loop(0, nf // 2, rd_body, 0)

    def vpart_copy(way):
        return pltpu.make_async_remote_copy(
            src_ref=vpart_send.at[way],
            dst_ref=vpart_recv.at[way],
            send_sem=vpart_sems.at[way, 0],
            recv_sem=vpart_sems.at[way, 1],
            device_id=along(2 * way - 1),
            device_id_type=MESH,
        )

    half = seg // 2

    def part_copy(way, e, upper=False):
        last = e == 2 * way
        lanes = pl.ds(half if upper else 0, half if last else seg)
        at = 3 if upper else e
        return pltpu.make_async_remote_copy(
            src_ref=part_send.at[way, e, :, lanes],
            dst_ref=part_recv.at[way, e, :, lanes],
            send_sem=part_sems.at[way, at, 0],
            recv_sem=part_sems.at[way, at, 1],
            device_id=along(2 * way - 1),
            device_id_type=MESH,
        )

    sends_to = (has_below, has_above)
    gets_from = (has_above, has_below)

    def start(copy, way):
        @pl.when(sends_to[way])
        def _():
            copy.start()

    def wait_recv(copy, way):
        @pl.when(gets_from[way])
        def _():
            copy.wait_recv()

    def wait_send(copy, way):
        @pl.when(sends_to[way])
        def _():
            copy.wait_send()

    a_lane = lax.broadcasted_iota(jnp.int32, (1, ka * width), 1)

    def columns_of(f):
        cols = [a_cols[k, f] for k in range(ka)]
        row = jnp.where(a_lane < width, cols[0], cols[1])
        for k in range(2, ka):
            row = jnp.where(a_lane >= k * width, cols[k], row)
        return cols, row

    def at_row(f):
        return pl.ds(pl.multiple_of(f * width, width), width)

    def near_body(i, carry):
        for t in range(WIDE):
            f = i * WIDE + t
            cols, row = columns_of(f)
            keep = jnp.where(row < nf, 1.0, 0.0).astype(BF16)
            table = jnp.concatenate([own[jnp.where(x < nf, x, 0)] for x in cols], axis=0)
            product = jnp.dot(a_ref[f] * keep, table, preferred_element_type=F32)
            appl[1, at_row(f), :] = product.astype(BF16)
        return carry

    inputs[3].wait()
    lax.fori_loop(0, nf // WIDE, near_body, 0)

    def restrict(e):
        terms = jnp.dot(rd[...], appl[e], preferred_element_type=F32)
        part_send[0, e] = terms[:seg].astype(BF16)
        own_part[e] = terms[seg : 2 * seg]
        part_send[1, e] = terms[2 * seg :].astype(BF16)

    restrict(1)
    vec_part = lax.dot_general(
        vec_t[...].astype(BF16),
        rd[...],
        (((1,), (1,)), ((), ())),
        preferred_element_type=F32,
    )
    vpart_send[0] = vec_part[:, 0:seg]
    vpart_send[1] = vec_part[:, 2 * seg : 3 * seg]
    vec_own = vec_part[:, seg : 2 * seg]
    @pl.when(has_below)
    def _():
        for copy in ghost_copies(1):
            copy.wait_recv()

    @pl.when(has_above)
    def _():
        for copy in ghost_copies(0):
            copy.wait_recv()

    for way in range(2):
        start(part_copy(way, 1), way)
    for way in range(2):
        start(vpart_copy(way), way)
    arrived_ghosts(1, 0)
    arrived_ghosts(0, gh)

    def far_body(i, carry):
        for t in range(WIDE):
            f = i * WIDE + t
            cols, row = columns_of(f)
            a_row = a_ref[f]
            low = jnp.where((row >= nf) & (row < nf + gh), 1.0, 0.0).astype(BF16)
            high = jnp.where(row >= nf + gh, 1.0, 0.0).astype(BF16)
            both = jnp.concatenate([a_row * low, a_row * high], axis=0)
            table = jnp.concatenate([ghost[jnp.where(x < nf, 0, x - nf)] for x in cols], axis=0)
            product = jnp.dot(both, table, preferred_element_type=F32).astype(BF16)
            appl[0, at_row(f), :] = product[:width]
            appl[2, at_row(f), :] = product[width:]
        return carry

    lax.fori_loop(0, nf // WIDE, far_body, 0)
    restrict(0)
    start(part_copy(1, 0), 1)
    restrict(2)
    start(part_copy(0, 2), 0)
    for upper in (False, True):
        start(part_copy(1, 2, upper), 1)
        start(part_copy(0, 0, upper), 0)

    owners = [dest[s] for s in range(nc)]
    ranks = []
    for s in range(nc):
        rank = jnp.int32(0)
        for before in range(s):
            rank = rank + jnp.where(owners[before] == owners[s], 1, 0)
        ranks.append(rank)
    sources = []
    for r in range(comp_count):
        to = lax.rem(c + r, comp_count)
        for k in range(cap):
            source = jnp.int32(nc)
            for s in range(nc):
                source = jnp.where((owners[s] == to) & (ranks[s] == k), s, source)
            sources.append(source)

    own_rows = pl.ds(c * cap, cap)

    pieces = [(0, 0, seg), (1, 0, seg), (2, 0, half), (3, 0, seg), (4, 0, seg), (2, half, half)]

    def slot_copy(piece, r):
        u, low, count = pieces[piece]
        return pltpu.make_async_remote_copy(
            src_ref=slots.at[u, r, :, :, pl.ds(low, count)],
            dst_ref=out_ref.at[own_rows, :, pl.ds(u * seg + low, count)],
            send_sem=slot_sems.at[piece, r - 1, 0],
            recv_sem=slot_sems.at[piece, r - 1, 1],
            device_id=peer(r),
            device_id_type=MESH,
        )

    def local_copy(piece):
        u, low, count = pieces[piece]
        return pltpu.make_async_copy(
            slots.at[u, 0, :, :, pl.ds(low, count)],
            out_ref.at[own_rows, :, pl.ds(u * seg + low, count)],
            local_sems.at[piece],
        )

    def finish(piece):
        u, low, count = pieces[piece]
        cut = slice(low, low + count)
        total = None
        if 1 <= u <= 3:
            total = own_part[u - 1, :, cut]
        if u >= 2:
            term = part_recv[0, u - 2, :, cut].astype(F32)
            total = term if total is None else total + term
        if u <= 2:
            term = part_recv[1, u, :, cut].astype(F32)
            total = term if total is None else total + term
        rounded = total.astype(BF16)
        for s in range(nc):
            rows[u, s, :, cut] = rounded[s * width : (s + 1) * width]
        rows[u, nc, :, cut] = jnp.zeros((width, count), BF16)
        for r in range(1, comp_count):
            for k in range(cap):
                slots[u, r, k, :, cut] = rows[u, sources[r * cap + k], :, cut]
            slot_copy(piece, r).start()
        for k in range(cap):
            slots[u, 0, k, :, cut] = rows[u, sources[k], :, cut]
        local_copy(piece).start()

    for way in range(2):
        wait_recv(vpart_copy(way), way)
    vec_total = vec_own + vpart_recv[0] + vpart_recv[1]
    vrows[...] = jnp.zeros_like(vrows)
    for s in range(nc):
        cut = slice(s * width, (s + 1) * width)
        both = jnp.concatenate([vec_total[0:1, cut], vec_total[1:2, cut]], axis=1)
        vrows[s, 0:1, :] = both
    for r in range(comp_count):
        picked = [vrows[sources[r * cap + k]] for k in range(cap)]
        for k in range(cap):
            vslots[r, k] = picked[k]

    def vslot_copy(r):
        return pltpu.make_async_remote_copy(
            src_ref=vslots.at[r],
            dst_ref=vslots_recv.at[r],
            send_sem=vslot_sems.at[r - 1, 0],
            recv_sem=vslot_sems.at[r - 1, 1],
            device_id=peer(r),
            device_id_type=MESH,
        )

    for r in range(1, comp_count):
        vslot_copy(r).start()

    wait_recv(part_copy(1, 1), 1)
    finish(1)
    wait_recv(part_copy(0, 1), 0)
    finish(3)
    wait_recv(part_copy(1, 0), 1)
    finish(0)
    wait_recv(part_copy(0, 2), 0)
    finish(4)
    wait_recv(part_copy(1, 2), 1)
    wait_recv(part_copy(0, 0), 0)
    finish(2)
    wait_recv(part_copy(1, 2, True), 1)
    wait_recv(part_copy(0, 0, True), 0)
    finish(5)

    vslots_recv[0] = vslots[0]
    for r in range(1, comp_count):
        vslot_copy(r).wait_recv()
    vec_rows = []
    for x in range(comp_count):
        for k in range(cap):
            row = jnp.zeros((1, 2 * width), F32)
            for r in range(comp_count):
                from_x = lax.rem(c + comp_count - r, comp_count) == x
                row = row + jnp.where(from_x, 1.0, 0.0) * vslots_recv[r, k, 0:1, :]
            vec_rows.append(row)
    out_vec[...] = jnp.concatenate(vec_rows, axis=0).astype(BF16)

    for piece in range(len(pieces)):
        for r in range(1, comp_count):
            slot_copy(piece, r).wait_recv()
        local_copy(piece).wait()
    for r in range(1, comp_count):
        vslot_copy(r).wait_send()
        for piece in range(len(pieces)):
            slot_copy(piece, r).wait_send()
    for way in range(2):
        wait_send(vpart_copy(way), way)
        for e in range(3):
            wait_send(part_copy(way, e), way)
        wait_send(part_copy(way, 2 * way, True), way)

    @pl.when(has_above)
    def _():
        for copy in ghost_copies(1):
            copy.wait_send()

    @pl.when(has_below)
    def _():
        for copy in ghost_copies(0):
            copy.wait_send()


def hand_on(matrix_in, vecs_in, matrix, vecs, sems):
    count = matrix_in.shape[0] // 2
    copies = [
        pltpu.make_async_copy(
            matrix_in.at[pl.ds(2 * i, 2)], matrix.at[pl.ds(2 * i, 2)], sems.at[i]
        )
        for i in range(count)
    ]
    copies.append(pltpu.make_async_copy(vecs_in, vecs, sems.at[count]))
    for copy in copies:
        copy.start()
    for copy in copies:
        copy.wait()


def on_device(
    mesh_count,
    comp_count,
    a_blocks,
    a_columns,
    p_blocks,
    p_columns,
    r_blocks,
    r_columns,
    sent_up,
    sent_down,
    vectors,
    coarse_dest,
):
    nf, width = a_blocks.shape[:2]
    ka, kp, kr = a_columns.shape[1], p_columns.shape[1], r_columns.shape[1]
    gh, nc = sent_up.shape[0], coarse_dest.shape[0]
    cap = max(2, nc // 2)
    seg = nc * width
    sizes = (mesh_count, comp_count, nf, width, ka, kp, kr, gh, nc, cap)
    smem = pl.BlockSpec(memory_space=pltpu.SMEM)
    hbm = pl.BlockSpec(memory_space=pl.ANY)
    vmem = pl.BlockSpec(memory_space=pltpu.VMEM)
    shapes = (
        jax.ShapeDtypeStruct((comp_count * cap, width, 5 * seg), BF16),
        jax.ShapeDtypeStruct((comp_count * cap, 2 * width), BF16),
    )
    found = pl.pallas_call(
        functools.partial(kernel, sizes),
        out_shape=shapes,
        in_specs=[smem] * 6 + [hbm] * 4,
        out_specs=(hbm, vmem),
        scratch_shapes=[
            pltpu.VMEM(a_blocks.shape, BF16),
            pltpu.VMEM(p_blocks.shape, BF16),
            pltpu.VMEM(r_blocks.shape, BF16),
            pltpu.VMEM(vectors.shape, BF16),
            pltpu.VMEM((nf, width, seg), BF16),
            pltpu.VMEM((2 * gh, width, seg), BF16),
            pltpu.VMEM((2, gh // 2, kp, width, 2 * width), BF16),
            pltpu.VMEM((2, gh // 2, kp, width, 2 * width), BF16),
            pltpu.VMEM((2, gh // 2, 8, 2 * width), F32),
            pltpu.VMEM((2, gh // 2, 8, 2 * width), F32),
            pltpu.VMEM((3 * seg, nf * width), BF16),
            pltpu.VMEM((3, nf * width, seg), BF16),
            pltpu.VMEM((2, 3, seg, seg), BF16),
            pltpu.VMEM((2, 3, seg, seg), BF16),
            pltpu.VMEM((3, seg, seg), F32),
            pltpu.VMEM((5, nc + 1, width, seg), BF16),
            pltpu.VMEM((5, comp_count, cap, width, seg), BF16),
            pltpu.VMEM((nf, 2 * width), F32),
            pltpu.VMEM((8, nf * width), F32),
            pltpu.VMEM((2, 8, seg), F32),
            pltpu.VMEM((2, 8, seg), F32),
            pltpu.VMEM((nc + 1, 8, 2 * width), F32),
            pltpu.VMEM((comp_count, cap, 8, 2 * width), F32),
            pltpu.VMEM((comp_count, cap, 8, 2 * width), F32),
            pltpu.SemaphoreType.DMA((2, 2, 2)),
            pltpu.SemaphoreType.DMA((2, 4, 2)),
            pltpu.SemaphoreType.DMA((2, 2)),
            pltpu.SemaphoreType.DMA((6, comp_count - 1, 2)),
            pltpu.SemaphoreType.DMA((6,)),
            pltpu.SemaphoreType.DMA((comp_count - 1, 2)),
            pltpu.SemaphoreType.DMA((4,)),
        ],
        compiler_params=pltpu.CompilerParams(
            collective_id=0, has_side_effects=True, vmem_limit_bytes=60 * 1024 * 1024
        ),
    )(
        a_columns.T,
        p_columns.T,
        r_columns.T,
        sent_up,
        sent_down,
        coarse_dest.reshape(nc),
        a_blocks,
        p_blocks,
        r_blocks,
        vectors,
    )
    return pl.pallas_call(
        hand_on,
        out_shape=shapes,
        in_specs=[hbm, hbm],
        out_specs=(hbm, hbm),
        scratch_shapes=[pltpu.SemaphoreType.DMA((comp_count * cap // 2 + 1,))],
        compiler_params=pltpu.CompilerParams(vmem_limit_bytes=60 * 1024 * 1024),
    )(*found)


def solution(mesh):
    placed = (
        P(("mesh", "comp"), None, None),
        P(("mesh", "comp"), None),
        P(("mesh", "comp"), None, None),
        P(("mesh", "comp"), None),
        P(("mesh", "comp"), None, None),
        P(("mesh", "comp"), None),
        P(("mesh", "comp")),
        P(("mesh", "comp")),
        P(("mesh", "comp"), None),
        P(("mesh", "comp"), None),
    )
    return jax.shard_map(
        functools.partial(on_device, mesh.shape["mesh"], mesh.shape["comp"]),
        mesh=mesh,
        in_specs=placed,
        out_specs=(P(("mesh", "comp"), None, None), P(("mesh", "comp"), None)),
        check_vma=False,
    )
```

```python
import functools

import jax
import jax.numpy as jnp
from jax import lax
from jax.experimental import pallas as pl
from jax.experimental.pallas import tpu as pltpu
from jax.sharding import PartitionSpec as P

MESH = pl.DeviceIdType.MESH
F32 = jnp.float32
BF16 = jnp.bfloat16
UNROLL = 4
WIDE = 8


def kernel(
    sizes,
    a_cols,
    p_cols,
    r_cols,
    up_rows,
    down_rows,
    dest,
    a_hbm,
    p_hbm,
    r_hbm,
    vec_hbm,
    out_ref,
    out_vec,
    a_ref,
    p_ref,
    r_ref,
    vec_ref,
    own,
    ghost,
    raw_send,
    raw_recv,
    name_send,
    name_recv,
    rd,
    appl,
    part_send,
    part_recv,
    own_part,
    rows,
    slots,
    vec_f32,
    vec_t,
    vpart_send,
    vpart_recv,
    vrows,
    vslots,
    vslots_recv,
    ghost_sems,
    part_sems,
    vpart_sems,
    slot_sems,
    local_sems,
    vslot_sems,
    in_sems,
):
    mesh_count, comp_count, nf, width, ka, kp, kr, gh, nc, cap = sizes
    seg = nc * width
    m = lax.axis_index("mesh")
    c = lax.axis_index("comp")
    has_below = m > 0
    has_above = m < mesh_count - 1

    def along(step):
        return (m + step, c)

    def peer(r):
        return (m, lax.rem(c + r, comp_count))

    inputs = [
        pltpu.make_async_copy(source, target, in_sems.at[i])
        for i, (source, target) in enumerate(
            ((p_hbm, p_ref), (r_hbm, r_ref), (vec_hbm, vec_ref), (a_hbm, a_ref))
        )
    ]
    for copy in inputs:
        copy.start()

    raw_recv[...] = jnp.zeros_like(raw_recv)
    name_recv[...] = jnp.zeros_like(name_recv)
    part_recv[...] = jnp.zeros_like(part_recv)
    vpart_recv[...] = jnp.zeros_like(vpart_recv)

    barrier = pltpu.get_barrier_semaphore()
    for r in range(1, comp_count):
        pl.semaphore_signal(barrier, inc=1, device_id=peer(r), device_id_type=MESH)

    @pl.when(has_above)
    def _():
        pl.semaphore_signal(barrier, inc=1, device_id=along(1), device_id_type=MESH)

    @pl.when(has_below)
    def _():
        pl.semaphore_signal(barrier, inc=1, device_id=along(-1), device_id_type=MESH)

    pair_lane = lax.broadcasted_iota(jnp.int32, (1, 2 * width), 1)
    first_half = pair_lane < width

    def twice(block):
        return jnp.concatenate([block, block], axis=1)

    def spread(blocks, names):
        tiles = []
        for s in range(0, nc, 2):
            here = jnp.where(first_half, s, s + 1).astype(F32)
            total = None
            for block, name in zip(blocks, names):
                term = block * jnp.where(here == name, 1.0, 0.0).astype(BF16)
                total = term if total is None else total + term
            tiles.append(total)
        return jnp.concatenate(tiles, axis=1)

    def dense_row(f):
        strip = p_ref[f]
        blocks = [twice(strip[:, q * width : (q + 1) * width]) for q in range(kp)]
        return spread(blocks, [p_cols[q, f].astype(F32) for q in range(kp)])

    def fill_ghosts(way, listed):
        def body(i, carry):
            rows_of = [listed[2 * i], listed[2 * i + 1]]
            strips = [p_ref[f] for f in rows_of]
            raw_send[way, i, 0] = strips[0][:, : 2 * width]
            raw_send[way, i, 1] = strips[1][:, : 2 * width]
            raw_send[way, i, 2] = jnp.concatenate([x[:, 2 * width :] for x in strips], axis=1)
            names = [
                jnp.zeros((1, 2 * width), F32) + p_cols[q, f].astype(F32)
                for f in rows_of
                for q in range(kp)
            ]
            names.append(jnp.zeros((8 - 2 * kp, 2 * width), F32))
            name_send[way, i] = jnp.concatenate(names, axis=0)
            return carry

        lax.fori_loop(0, gh // 2, body, 0)

    def ghost_copies(way):
        return [
            pltpu.make_async_remote_copy(
                src_ref=source.at[way],
                dst_ref=target.at[way],
                send_sem=ghost_sems.at[way, i, 0],
                recv_sem=ghost_sems.at[way, i, 1],
                device_id=along(2 * way - 1),
                device_id_type=MESH,
            )
            for i, (source, target) in enumerate(((raw_send, raw_recv), (name_send, name_recv)))
        ]

    def arrived_ghosts(way, at):
        def body(i, carry):
            last = raw_recv[way, i, 2]
            for t in range(2):
                pair = raw_recv[way, i, t]
                blocks = [
                    twice(pair[:, :width]),
                    twice(pair[:, width:]),
                    twice(last[:, t * width : (t + 1) * width]),
                ]
                names = [name_recv[way, i, t * kp + q : t * kp + q + 1, :] for q in range(kp)]
                ghost[at + 2 * i + t] = spread(blocks, names)
            return carry

        lax.fori_loop(0, gh // 2, body, 0)

    inputs[0].wait()
    fill_ghosts(1, up_rows)
    pl.semaphore_wait(
        barrier,
        comp_count - 1 + jnp.where(has_below, 1, 0) + jnp.where(has_above, 1, 0),
    )

    @pl.when(has_above)
    def _():
        for copy in ghost_copies(1):
            copy.start()

    fill_ghosts(0, down_rows)

    @pl.when(has_below)
    def _():
        for copy in ghost_copies(0):
            copy.start()

    def own_body(i, carry):
        for t in range(UNROLL):
            f = i * UNROLL + t
            own[f] = dense_row(f)
        return carry

    lax.fori_loop(0, nf // UNROLL, own_body, 0)

    inputs[1].wait()
    inputs[2].wait()
    vec_f32[...] = vec_ref[...].astype(F32)
    vec_t[...] = jnp.zeros_like(vec_t)
    def rd_body(i, carry):
        f = i * 2
        at = pl.ds(pl.multiple_of(i * 2 * width, 2 * width), 2 * width)
        even = r_ref[f]
        odd = r_ref[f + 1]
        blocks = []
        named = []
        for j in range(kr):
            cut = slice(j * width, (j + 1) * width)
            blocks.append(jnp.concatenate([even[:, cut], odd[:, cut]], axis=1))
            named.append(jnp.where(first_half, r_cols[j, f], r_cols[j, f + 1]))
        for target in range(3 * nc):
            total = None
            for j in range(kr):
                hit = jnp.where(named[j] == target, 1.0, 0.0).astype(BF16)
                term = blocks[j] * hit
                total = term if total is None else total + term
            rd[target * width : (target + 1) * width, at] = total
        v0 = vec_f32[pl.ds(f, 1), :]
        v1 = vec_f32[pl.ds(f + 1, 1), :]
        vec_t[0:1, at] = jnp.where(first_half, v0, pltpu.roll(v1, width, 1))
        vec_t[1:2, at] = jnp.where(first_half, pltpu.roll(v0, width, 1), v1)
        return carry

    lax.fori_loop(0, nf // 2, rd_body, 0)

    def vpart_copy(way):
        return pltpu.make_async_remote_copy(
            src_ref=vpart_send.at[way],
            dst_ref=vpart_recv.at[way],
            send_sem=vpart_sems.at[way, 0],
            recv_sem=vpart_sems.at[way, 1],
            device_id=along(2 * way - 1),
            device_id_type=MESH,
        )

    def part_copy(way, e):
        return pltpu.make_async_remote_copy(
            src_ref=part_send.at[way, e],
            dst_ref=part_recv.at[way, e],
            send_sem=part_sems.at[way, e, 0],
            recv_sem=part_sems.at[way, e, 1],
            device_id=along(2 * way - 1),
            device_id_type=MESH,
        )

    sends_to = (has_below, has_above)
    gets_from = (has_above, has_below)

    def start(copy, way):
        @pl.when(sends_to[way])
        def _():
            copy.start()

    def wait_recv(copy, way):
        @pl.when(gets_from[way])
        def _():
            copy.wait_recv()

    def wait_send(copy, way):
        @pl.when(sends_to[way])
        def _():
            copy.wait_send()

    a_lane = lax.broadcasted_iota(jnp.int32, (1, ka * width), 1)

    def columns_of(f):
        cols = [a_cols[k, f] for k in range(ka)]
        row = jnp.where(a_lane < width, cols[0], cols[1])
        for k in range(2, ka):
            row = jnp.where(a_lane >= k * width, cols[k], row)
        return cols, row

    def at_row(f):
        return pl.ds(pl.multiple_of(f * width, width), width)

    def near_body(i, carry):
        for t in range(WIDE):
            f = i * WIDE + t
            cols, row = columns_of(f)
            keep = jnp.where(row < nf, 1.0, 0.0).astype(BF16)
            table = jnp.concatenate([own[jnp.where(x < nf, x, 0)] for x in cols], axis=0)
            product = jnp.dot(a_ref[f] * keep, table, preferred_element_type=F32)
            appl[1, at_row(f), :] = product.astype(BF16)
        return carry

    inputs[3].wait()
    lax.fori_loop(0, nf // WIDE, near_body, 0)

    def restrict(e):
        terms = jnp.dot(rd[...], appl[e], preferred_element_type=F32)
        part_send[0, e] = terms[:seg].astype(BF16)
        own_part[e] = terms[seg : 2 * seg]
        part_send[1, e] = terms[2 * seg :].astype(BF16)

    restrict(1)
    vec_part = lax.dot_general(
        vec_t[...].astype(BF16),
        rd[...],
        (((1,), (1,)), ((), ())),
        preferred_element_type=F32,
    )
    vpart_send[0] = vec_part[:, 0:seg]
    vpart_send[1] = vec_part[:, 2 * seg : 3 * seg]
    vec_own = vec_part[:, seg : 2 * seg]
    @pl.when(has_below)
    def _():
        for copy in ghost_copies(1):
            copy.wait_recv()

    @pl.when(has_above)
    def _():
        for copy in ghost_copies(0):
            copy.wait_recv()

    for way in range(2):
        start(part_copy(way, 1), way)
    for way in range(2):
        start(vpart_copy(way), way)
    arrived_ghosts(1, 0)
    arrived_ghosts(0, gh)

    def far_body(i, carry):
        for t in range(WIDE):
            f = i * WIDE + t
            cols, row = columns_of(f)
            a_row = a_ref[f]
            low = jnp.where((row >= nf) & (row < nf + gh), 1.0, 0.0).astype(BF16)
            high = jnp.where(row >= nf + gh, 1.0, 0.0).astype(BF16)
            both = jnp.concatenate([a_row * low, a_row * high], axis=0)
            table = jnp.concatenate([ghost[jnp.where(x < nf, 0, x - nf)] for x in cols], axis=0)
            product = jnp.dot(both, table, preferred_element_type=F32).astype(BF16)
            appl[0, at_row(f), :] = product[:width]
            appl[2, at_row(f), :] = product[width:]
        return carry

    lax.fori_loop(0, nf // WIDE, far_body, 0)
    restrict(0)
    start(part_copy(1, 0), 1)
    restrict(2)
    start(part_copy(0, 2), 0)
    start(part_copy(1, 2), 1)
    start(part_copy(0, 0), 0)

    owners = [dest[s] for s in range(nc)]
    ranks = []
    for s in range(nc):
        rank = jnp.int32(0)
        for before in range(s):
            rank = rank + jnp.where(owners[before] == owners[s], 1, 0)
        ranks.append(rank)
    sources = []
    for r in range(comp_count):
        to = lax.rem(c + r, comp_count)
        for k in range(cap):
            source = jnp.int32(nc)
            for s in range(nc):
                source = jnp.where((owners[s] == to) & (ranks[s] == k), s, source)
            sources.append(source)

    own_rows = pl.ds(c * cap, cap)

    def slot_copy(u, r):
        return pltpu.make_async_remote_copy(
            src_ref=slots.at[u, r],
            dst_ref=out_ref.at[own_rows, :, pl.ds(u * seg, seg)],
            send_sem=slot_sems.at[u, r - 1, 0],
            recv_sem=slot_sems.at[u, r - 1, 1],
            device_id=peer(r),
            device_id_type=MESH,
        )

    def local_copy(u):
        return pltpu.make_async_copy(
            slots.at[u, 0], out_ref.at[own_rows, :, pl.ds(u * seg, seg)], local_sems.at[u]
        )

    def finish(u):
        total = None
        if 1 <= u <= 3:
            total = own_part[u - 1]
        if u >= 2:
            term = part_recv[0, u - 2].astype(F32)
            total = term if total is None else total + term
        if u <= 2:
            term = part_recv[1, u].astype(F32)
            total = term if total is None else total + term
        rounded = total.astype(BF16)
        for s in range(nc):
            rows[u, s] = rounded[s * width : (s + 1) * width]
        rows[u, nc] = jnp.zeros((width, seg), BF16)
        for r in range(1, comp_count):
            for k in range(cap):
                slots[u, r, k] = rows[u, sources[r * cap + k]]
            slot_copy(u, r).start()
        for k in range(cap):
            slots[u, 0, k] = rows[u, sources[k]]
        local_copy(u).start()

    for way in range(2):
        wait_recv(vpart_copy(way), way)
    vec_total = vec_own + vpart_recv[0] + vpart_recv[1]
    vrows[...] = jnp.zeros_like(vrows)
    for s in range(nc):
        cut = slice(s * width, (s + 1) * width)
        both = jnp.concatenate([vec_total[0:1, cut], vec_total[1:2, cut]], axis=1)
        vrows[s, 0:1, :] = both
    for r in range(comp_count):
        picked = [vrows[sources[r * cap + k]] for k in range(cap)]
        for k in range(cap):
            vslots[r, k] = picked[k]

    def vslot_copy(r):
        return pltpu.make_async_remote_copy(
            src_ref=vslots.at[r],
            dst_ref=vslots_recv.at[r],
            send_sem=vslot_sems.at[r - 1, 0],
            recv_sem=vslot_sems.at[r - 1, 1],
            device_id=peer(r),
            device_id_type=MESH,
        )

    for r in range(1, comp_count):
        vslot_copy(r).start()

    wait_recv(part_copy(1, 1), 1)
    finish(1)
    wait_recv(part_copy(0, 1), 0)
    finish(3)
    wait_recv(part_copy(1, 0), 1)
    finish(0)
    wait_recv(part_copy(0, 2), 0)
    finish(4)
    wait_recv(part_copy(1, 2), 1)
    wait_recv(part_copy(0, 0), 0)
    finish(2)

    vslots_recv[0] = vslots[0]
    for r in range(1, comp_count):
        vslot_copy(r).wait_recv()
    vec_rows = []
    for x in range(comp_count):
        for k in range(cap):
            row = jnp.zeros((1, 2 * width), F32)
            for r in range(comp_count):
                from_x = lax.rem(c + comp_count - r, comp_count) == x
                row = row + jnp.where(from_x, 1.0, 0.0) * vslots_recv[r, k, 0:1, :]
            vec_rows.append(row)
    out_vec[...] = jnp.concatenate(vec_rows, axis=0).astype(BF16)

    for u in range(5):
        for r in range(1, comp_count):
            slot_copy(u, r).wait_recv()
        local_copy(u).wait()
    for r in range(1, comp_count):
        vslot_copy(r).wait_send()
        for u in range(5):
            slot_copy(u, r).wait_send()
    for way in range(2):
        wait_send(vpart_copy(way), way)
        for e in range(3):
            wait_send(part_copy(way, e), way)

    @pl.when(has_above)
    def _():
        for copy in ghost_copies(1):
            copy.wait_send()

    @pl.when(has_below)
    def _():
        for copy in ghost_copies(0):
            copy.wait_send()


def hand_on(matrix_in, vecs_in, matrix, vecs, held, held_vecs, sems):
    count = held.shape[0] // 2
    loads = [pltpu.make_async_copy(vecs_in, held_vecs, sems.at[0, count])]
    stores = [pltpu.make_async_copy(held_vecs, vecs, sems.at[1, count])]
    for i in range(count):
        part = pl.ds(2 * i, 2)
        loads.append(pltpu.make_async_copy(matrix_in.at[part], held.at[part], sems.at[0, i]))
        stores.append(pltpu.make_async_copy(held.at[part], matrix.at[part], sems.at[1, i]))
    for load in loads:
        load.start()
    for load, store in zip(loads, stores):
        load.wait()
        store.start()
    for store in stores:
        store.wait()


def on_device(
    mesh_count,
    comp_count,
    a_blocks,
    a_columns,
    p_blocks,
    p_columns,
    r_blocks,
    r_columns,
    sent_up,
    sent_down,
    vectors,
    coarse_dest,
):
    nf, width = a_blocks.shape[:2]
    ka, kp, kr = a_columns.shape[1], p_columns.shape[1], r_columns.shape[1]
    gh, nc = sent_up.shape[0], coarse_dest.shape[0]
    cap = max(2, nc // 2)
    seg = nc * width
    sizes = (mesh_count, comp_count, nf, width, ka, kp, kr, gh, nc, cap)
    smem = pl.BlockSpec(memory_space=pltpu.SMEM)
    hbm = pl.BlockSpec(memory_space=pl.ANY)
    vmem = pl.BlockSpec(memory_space=pltpu.VMEM)
    shapes = (
        jax.ShapeDtypeStruct((comp_count * cap, width, 5 * seg), BF16),
        jax.ShapeDtypeStruct((comp_count * cap, 2 * width), BF16),
    )
    found = pl.pallas_call(
        functools.partial(kernel, sizes),
        out_shape=shapes,
        in_specs=[smem] * 6 + [hbm] * 4,
        out_specs=(hbm, vmem),
        scratch_shapes=[
            pltpu.VMEM(a_blocks.shape, BF16),
            pltpu.VMEM(p_blocks.shape, BF16),
            pltpu.VMEM(r_blocks.shape, BF16),
            pltpu.VMEM(vectors.shape, BF16),
            pltpu.VMEM((nf, width, seg), BF16),
            pltpu.VMEM((2 * gh, width, seg), BF16),
            pltpu.VMEM((2, gh // 2, kp, width, 2 * width), BF16),
            pltpu.VMEM((2, gh // 2, kp, width, 2 * width), BF16),
            pltpu.VMEM((2, gh // 2, 8, 2 * width), F32),
            pltpu.VMEM((2, gh // 2, 8, 2 * width), F32),
            pltpu.VMEM((3 * seg, nf * width), BF16),
            pltpu.VMEM((3, nf * width, seg), BF16),
            pltpu.VMEM((2, 3, seg, seg), BF16),
            pltpu.VMEM((2, 3, seg, seg), BF16),
            pltpu.VMEM((3, seg, seg), F32),
            pltpu.VMEM((5, nc + 1, width, seg), BF16),
            pltpu.VMEM((5, comp_count, cap, width, seg), BF16),
            pltpu.VMEM((nf, 2 * width), F32),
            pltpu.VMEM((8, nf * width), F32),
            pltpu.VMEM((2, 8, seg), F32),
            pltpu.VMEM((2, 8, seg), F32),
            pltpu.VMEM((nc + 1, 8, 2 * width), F32),
            pltpu.VMEM((comp_count, cap, 8, 2 * width), F32),
            pltpu.VMEM((comp_count, cap, 8, 2 * width), F32),
            pltpu.SemaphoreType.DMA((2, 2, 2)),
            pltpu.SemaphoreType.DMA((2, 3, 2)),
            pltpu.SemaphoreType.DMA((2, 2)),
            pltpu.SemaphoreType.DMA((5, comp_count - 1, 2)),
            pltpu.SemaphoreType.DMA((5,)),
            pltpu.SemaphoreType.DMA((comp_count - 1, 2)),
            pltpu.SemaphoreType.DMA((4,)),
        ],
        compiler_params=pltpu.CompilerParams(
            collective_id=0, has_side_effects=True, vmem_limit_bytes=60 * 1024 * 1024
        ),
    )(
        a_columns.T,
        p_columns.T,
        r_columns.T,
        sent_up,
        sent_down,
        coarse_dest.reshape(nc),
        a_blocks,
        p_blocks,
        r_blocks,
        vectors,
    )
    return pl.pallas_call(
        hand_on,
        out_shape=shapes,
        in_specs=[hbm, hbm],
        out_specs=(hbm, hbm),
        scratch_shapes=[
            pltpu.VMEM(shapes[0].shape, BF16),
            pltpu.VMEM(shapes[1].shape, BF16),
            pltpu.SemaphoreType.DMA((2, comp_count * cap // 2 + 1)),
        ],
        compiler_params=pltpu.CompilerParams(vmem_limit_bytes=60 * 1024 * 1024),
    )(*found)


def solution(mesh):
    placed = (
        P(("mesh", "comp"), None, None),
        P(("mesh", "comp"), None),
        P(("mesh", "comp"), None, None),
        P(("mesh", "comp"), None),
        P(("mesh", "comp"), None, None),
        P(("mesh", "comp"), None),
        P(("mesh", "comp")),
        P(("mesh", "comp")),
        P(("mesh", "comp"), None),
        P(("mesh", "comp"), None),
    )
    return jax.shard_map(
        functools.partial(on_device, mesh.shape["mesh"], mesh.shape["comp"]),
        mesh=mesh,
        in_specs=placed,
        out_specs=(P(("mesh", "comp"), None, None), P(("mesh", "comp"), None)),
        check_vma=False,
    )
```
